128 devices in a mesh: ctx: 64 (over x_hi, y, z, core), head: 2 (over x_lo).
Axes of the slice: x: 4 (x_hi: 2, x_lo: 2; x = x_hi * 2 + x_lo), y: 4, z: 4, core: 2. Of those that a mesh axis runs over, the one named last changes fastest.
Arguments:
- queries: bfloat16 [2, 10240, 2048], P(None, 'ctx', 'head'), may hold values from -8 to 100
- keys: bfloat16 [2, 10240, 512], P(None, 'ctx', 'head'), may hold values from -8 to 8
- values: bfloat16 [2, 10240, 512], P(None, 'ctx', 'head'), may hold values from -6 to 6
- doc_start: int32 [10240], P('ctx'), may hold values from 0 to 8320, as said below
- out_weight: bfloat16 [2, 2048, 4096], P(None, None, 'head'), may hold values from -0.25 to 0.25
Outputs:
- attended: bfloat16 [2, 10240, 4096], P(None, 'ctx', 'head')
The draws below stay inside these ranges and needn't reach their ends.
Inputs may be any that keep to these rules, and one draw needn't show every extreme that they name: doc_start[i] is the position of the first token of the document holding row i's token; the 4 documents lie one after another from position 0, so doc_start[i] <= pos[i]; the last document starts at position (3) * 2560 + 10240 // 16.
All inputs are finite; a program needn't handle non-finite values.
Results may differ from the reference program's by a relative error of at most 0.012.
The reference program's roundings to bfloat16 on the way count: a program that leaves them out, or rounds other values in their place, can miss the bound.
Values may be sent and summed in bfloat16 or wider, within the bound.
A program may use at most 128 MiB of HBM per device.

```python
import math
import jax
import jax.numpy as jnp
import numpy as np
from jax import lax

D = 4096
HD = 128
QH = 16
KVH = 4
MODELS = 2
DOCS = 4
TOK_DEV = 160
STRIPES = 64
TOKENS = 10240


def draw_queries(key, part):
    key = jax.random.fold_in(key, 11)
    drawn = jnp.clip(1.75 * jax.random.normal(key, (MODELS, TOKENS, QH * HD), jnp.float32), -8.0, 8.0)
    return drawn.astype(jnp.bfloat16)


def draw_keys(key, part):
    key = jax.random.fold_in(key, 23)
    drawn = jnp.clip(1.75 * jax.random.normal(key, (MODELS, TOKENS, KVH * HD), jnp.float32), -8.0, 8.0)
    return drawn.astype(jnp.bfloat16)


def draw_doc_start(key, part):
    key = jax.random.fold_in(key, 37)
    spread = TOKENS // (4 * DOCS)
    offsets = jax.random.randint(key, (DOCS - 1,), -spread, spread + 1)
    offsets = offsets.at[DOCS - 2].set(spread)
    cut_points = (jnp.arange(1, DOCS, dtype=jnp.int32) * (TOKENS // DOCS) + offsets).astype(jnp.int32)
    places = jnp.arange(TOKENS, dtype=jnp.int32)
    starts = jnp.max(jnp.where(places[:, None] >= cut_points[None, :], cut_points[None, :], 0), axis=1)
    return starts.reshape(TOK_DEV, STRIPES).T.reshape(TOKENS).astype(jnp.int32)


def block_scale(own_key, dims, pieces, low, high):
    def one(axis_at, parts):
        steps = jax.random.uniform(jax.random.fold_in(jax.random.fold_in(own_key, 6), axis_at), (parts,), jnp.float32, low / len(pieces), high / len(pieces))
        return jnp.repeat(jnp.exp(steps), dims[axis_at] // parts).reshape((-1,) + (1,) * (len(dims) - axis_at - 1))

    gain = one(*pieces[0])
    for cut in pieces[1:]:
        gain = gain * one(*cut)
    return gain


def centred(own_key, dims, scale, reach, cuts=(), kind=jnp.bfloat16):
    gain = block_scale(own_key, dims, cuts, -0.22, 0.18) if cuts else 1.0
    entries = jax.random.normal(own_key, dims, jnp.float32) * scale * gain
    return jnp.minimum(jnp.maximum(entries, -reach), reach).astype(kind)


def setup_inputs(seed: int = 0) -> dict:
    arg_keys = jax.random.split(jax.random.key(seed), 6)
    return {
        "queries": draw_queries(jax.random.fold_in(arg_keys[5], 71), 0),
        "keys": draw_keys(jax.random.fold_in(arg_keys[5], 71), 0),
        "values": centred(arg_keys[2], (MODELS, TOKENS, KVH * HD), 1.0, 6.0, ((1, 64), (2, 2))),
        "doc_start": draw_doc_start(jax.random.fold_in(arg_keys[5], 71), 0),
        "out_weight": centred(arg_keys[4], (MODELS, QH * HD, D), (QH * HD // 4) ** -0.5, 0.25, ((2, 2),)),
    }


def rotate_pairs(tensor, positions, head_width):
    half_width = head_width // 2
    inverse_freq = jnp.asarray(np.power(500000.0, -np.arange(half_width) * 2.0 / head_width).astype(np.float32))
    angles = positions.astype(jnp.float32)[:, None] * inverse_freq[None, :]
    cosine = jnp.cos(angles)[None, :, None, :]
    sine_part = jnp.sin(angles)[None, :, None, :]
    models, length, total_width = tensor.shape
    split_view = tensor.astype(jnp.float32).reshape(models, length, total_width // head_width, 2, half_width)
    first_half = split_view[:, :, :, 0, :]
    second_half = split_view[:, :, :, 1, :]
    turned = jnp.stack([first_half * cosine - second_half * sine_part, second_half * cosine + first_half * sine_part], axis=3)
    return turned.reshape(models, length, total_width).astype(jnp.bfloat16)


def reference(queries, keys, values, doc_start, out_weight):
    row_ids = jnp.arange(TOKENS, dtype=jnp.int32)
    positions = (row_ids % TOK_DEV) * STRIPES + row_ids // TOK_DEV
    queries_rot = rotate_pairs(queries, positions, HD)
    keys_rot = rotate_pairs(keys, positions, HD)
    group_size = QH // KVH
    key_view = keys_rot.reshape(MODELS, TOKENS, KVH, HD).astype(jnp.float32)
    value_view = values.reshape(MODELS, TOKENS, KVH, HD).astype(jnp.float32)
    block_rows = math.gcd(TOKENS, 128)

    def one_block(block_index):
        start_row = (block_index * block_rows).astype(jnp.int32)
        query_view = lax.dynamic_slice_in_dim(queries_rot, start_row, block_rows, 1)
        query_view = query_view.reshape(MODELS, block_rows, KVH, group_size, HD).astype(jnp.float32)
        query_pos = lax.dynamic_slice_in_dim(positions, start_row, block_rows)
        doc_first = lax.dynamic_slice_in_dim(doc_start, start_row, block_rows)
        scores = jnp.einsum("mtgrd,mkgd->mgrtk", query_view, key_view, precision=lax.Precision.HIGHEST) * (HD ** -0.5)
        allowed = (positions[None, :] <= query_pos[:, None]) & (positions[None, :] >= doc_first[:, None])
        masked = jnp.where(allowed, scores, -1e30)
        row_max = jnp.max(masked, axis=-1, keepdims=True)
        weights = jnp.where(allowed, jnp.exp(scores - row_max), 0.0)
        row_sum = jnp.sum(weights, axis=-1)
        rounded = lax.optimization_barrier(weights.astype(jnp.bfloat16)).astype(jnp.float32)
        context = jnp.einsum("mgrtk,mkgd->mtgrd", rounded, value_view, precision=lax.Precision.HIGHEST)
        context = context / jnp.transpose(row_sum, (0, 3, 1, 2))[..., None]
        return context.reshape(MODELS, block_rows, QH * HD).astype(jnp.bfloat16)

    blocks = lax.map(one_block, jnp.arange(TOKENS // block_rows, dtype=jnp.int32))
    context = jnp.transpose(blocks, (1, 0, 2, 3)).reshape(MODELS, TOKENS, QH * HD)
    attended = jnp.stack([jnp.dot(context[model_index], out_weight[model_index], preferred_element_type=jnp.float32) for model_index in range(MODELS)])
    return attended.astype(jnp.bfloat16)
```

```python
import functools

import jax
import jax.numpy as jnp
import numpy as np
from jax import lax
from jax.experimental import pallas as pl
from jax.experimental.pallas import tpu as pltpu
from jax.sharding import PartitionSpec as P

MESH = pl.DeviceIdType.MESH
HD = 128
NY, NZ = 4, 4
TOK = 160
STRIPES = 64
GROUP = 4
TILE = 16
BLOCKS = TOK // TILE
KEYS = TILE * STRIPES
ROWS = NY * GROUP * TILE
LOW = -1e30
LOG2E = 1.4426950408889634


def place():
    c = lax.axis_index("ctx")
    return c // 32, (c // 8) % NY, (c // 2) % NZ, c % 2, lax.axis_index("head")


def index(xh, y, z, core):
    return ((xh * NY + y) * NZ + z) * 2 + core


def enter(partners):
    barrier = pltpu.get_barrier_semaphore()
    for device in partners:
        pl.semaphore_signal(barrier, inc=1, device_id=device, device_id_type=MESH)
    return barrier


def rotated(x, cosine, sine):
    x = x.astype(jnp.float32)
    return (x * cosine + pltpu.roll(x, 64, 1) * sine).astype(jnp.bfloat16)


def gather_kernel(
    freq_ref, q_ref, k_ref, v_ref, doc_ref, kv, q_out, doc_out,
    stage, xstage, qstage, tables, send, recv, xrecv, qrecv, drecv, local,
):
    xh, y, z, core, head = place()
    me = index(xh, y, z, core)
    xpart = index(1 - xh, y, z, core)
    ypeer = [index(xh, (y + d) % NY, z, core) for d in range(NY)]
    zup, zdown = index(xh, y, (z + 1) % NZ, core), index(xh, y, (z + 3) % NZ, core)
    sibling = index(xh, y, z, 1 - core)
    partners = [xpart, ypeer[1], ypeer[2], ypeer[3], zup, zdown, sibling]
    barrier = enter([(p, head) for p in partners])

    positions = lax.broadcasted_iota(jnp.int32, (TOK, HD), 0) * STRIPES + me
    angles = positions.astype(jnp.float32) * freq_ref[...]
    first = lax.broadcasted_iota(jnp.int32, (TOK, HD), 1) < HD // 2
    sine = jnp.sin(angles)
    tables[0] = jnp.cos(angles)
    tables[1] = jnp.where(first, -sine, sine)

    for p in range(4):
        cols = pl.ds(p % 2 * HD, HD)
        stage[p, 0] = rotated(k_ref[p // 2, :, cols], tables[0], tables[1])
        stage[p, 1] = v_ref[p // 2, :, cols]
    pl.semaphore_wait(barrier, len(partners))

    started = []

    def push(src, dst, sem, device):
        copy = pltpu.make_async_remote_copy(
            src_ref=src, dst_ref=dst, send_sem=send.at[len(started)], recv_sem=sem,
            device_id=(device, head), device_id_type=MESH,
        )
        copy.start()
        started.append(copy)

    def arrived(dst, sem):
        pltpu.make_async_remote_copy(
            src_ref=dst, dst_ref=dst, send_sem=send.at[0], recv_sem=sem,
            device_id=(sibling, head), device_id_type=MESH,
        ).wait_recv()

    def slot(k, zz, cc):
        return index(xh if k < 4 else 1 - xh, (y + k) % NY, zz, cc)

    def forward(s, device):
        push(kv.at[s], kv.at[s], recv.at[s], device)

    def take(k, zz):
        s = slot(k, zz, core)
        arrived(kv.at[s], recv.at[s])
        return s

    own = stage.at[y]
    push(own, kv.at[me], recv.at[me], zup)
    push(own, kv.at[me], recv.at[me], zdown)
    push(own, kv.at[me], recv.at[me], xpart)
    for d in (2, 1, 3):
        push(stage.at[(y + d) % NY], kv.at[me], recv.at[me], ypeer[d])
    for d in (1, 2, 3):
        push(stage.at[(y + d) % NY], xstage.at[d - 1], xrecv.at[d - 1], xpart)
    push(own, kv.at[me], recv.at[me], sibling)
    own_copy = pltpu.make_async_copy(own, kv.at[me], local.at[0])
    own_copy.start()

    for p in range(4):
        for r in range(GROUP):
            cols = pl.ds((p % 2 * GROUP + r) * HD, HD)
            qstage[p, :, pl.ds(r * HD, HD)] = rotated(q_ref[p // 2, :, cols], tables[0], tables[1])
    q_copy = pltpu.make_async_copy(qstage.at[y], q_out.at[y], local.at[1])
    q_copy.start()
    doc_copy = pltpu.make_async_copy(doc_ref, doc_out.at[y], local.at[2])
    doc_copy.start()

    zn, zp, zo = (z + 1) % NZ, (z + 3) % NZ, (z + 2) % NZ
    for k in range(8):
        if k > 0:
            s = take(k, z)
            forward(s, zup)
            forward(s, zdown)
            forward(s, sibling)
        s = take(k, zp)
        if k % 2 == 0:
            forward(s, zup)
        forward(s, sibling)
        s = take(k, zn)
        if k % 2 == 1:
            forward(s, zdown)
        forward(s, sibling)
        if k > 0:
            forward(take(k - 1, zo), sibling)
        if k == 2:
            for d in (1, 2, 3):
                arrived(xstage.at[d - 1], xrecv.at[d - 1])
                push(xstage.at[d - 1], kv.at[xpart], recv.at[xpart], ypeer[d])
            for d in (2, 1, 3):
                push(qstage.at[(y + d) % NY], q_out.at[y], qrecv.at[y], ypeer[d])
                push(doc_ref, doc_out.at[y], drecv.at[y], ypeer[d])
    forward(take(7, zo), sibling)
    for k in range(8):
        for zz in (z, zp, zn, zo):
            s = slot(k, zz, 1 - core)
            arrived(kv.at[s], recv.at[s])
    for d in (1, 2, 3):
        p = (y + d) % NY
        arrived(q_out.at[p], qrecv.at[p])
        arrived(doc_out.at[p], drecv.at[p])
    own_copy.wait()
    q_copy.wait()
    doc_copy.wait()
    for copy in started:
        copy.wait_send()


def gather(freq, q, k, v, doc):
    vmem = pl.BlockSpec(memory_space=pltpu.VMEM)
    hbm = pl.BlockSpec(memory_space=pl.ANY)
    dma = pltpu.SemaphoreType.DMA
    return pl.pallas_call(
        gather_kernel,
        out_shape=(
            jax.ShapeDtypeStruct((STRIPES, 2, TOK, HD), jnp.bfloat16),
            jax.ShapeDtypeStruct((NY, TOK, GROUP * HD), jnp.bfloat16),
            jax.ShapeDtypeStruct((NY, TOK, HD), jnp.int32),
        ),
        in_specs=[vmem] * 5,
        out_specs=(hbm, hbm, hbm),
        scratch_shapes=[
            pltpu.VMEM((4, 2, TOK, HD), jnp.bfloat16),
            pltpu.VMEM((3, 2, TOK, HD), jnp.bfloat16),
            pltpu.VMEM((4, TOK, GROUP * HD), jnp.bfloat16),
            pltpu.VMEM((2, TOK, HD), jnp.float32),
            dma((96,)),
            dma((STRIPES,)),
            dma((3,)),
            dma((NY,)),
            dma((NY,)),
            dma((3,)),
        ],
        compiler_params=pltpu.CompilerParams(
            collective_id=0, has_side_effects=True, vmem_limit_bytes=32 * 2**20
        ),
    )(freq, q, k, v, doc)


def attend_kernel(kv_hbm, q_ref, doc_ref, out_ref, kbuf, vbuf, qbuf, top, total, acc, sem):
    xh, y, z, core, _ = place()
    copies = []
    for j in range(BLOCKS):
        rows = pl.ds(j * TILE, TILE)
        pair = (
            pltpu.make_async_copy(kv_hbm.at[:, 0, rows], kbuf.at[j], sem.at[0, j]),
            pltpu.make_async_copy(kv_hbm.at[:, 1, rows], vbuf.at[j], sem.at[1, j]),
        )
        for copy in pair:
            copy.start()
        copies.append(pair)

    lane = lax.broadcasted_iota(jnp.int32, (1, KEYS), 1)
    key_at = (lane % TILE) * STRIPES + lane // TILE
    scale = HD**-0.5 * LOG2E

    for i in range(BLOCKS):
        for copy in copies[i]:
            copy.wait()
        rows = pl.ds(i * TILE, TILE)
        docs = doc_ref[:, rows, :]
        low_doc = jnp.min(docs.astype(jnp.float32)).astype(jnp.int32)
        high_doc = jnp.max(docs.astype(jnp.float32)).astype(jnp.int32)
        for src in range(NY):
            for r in range(GROUP):
                at = (src * GROUP + r) * TILE
                qbuf[pl.ds(at, TILE), :] = q_ref[src, rows, pl.ds(r * HD, HD)]
        top[...] = jnp.full_like(top, LOW)
        total[...] = jnp.zeros_like(total)
        acc[...] = jnp.zeros_like(acc)

        def step(j, masked):
            keys = kbuf[j].reshape(KEYS, HD)
            values = vbuf[j].reshape(KEYS, HD)
            scores = lax.dot_general(
                qbuf[...], keys, (((1,), (1,)), ((), ())), preferred_element_type=jnp.float32
            ) * scale
            if masked:
                key_pos = key_at + j * (TILE * STRIPES)
                allowed = []
                for src in range(NY):
                    t = lax.broadcasted_iota(jnp.int32, (TILE, 1), 0) + i * TILE
                    q_pos = t * STRIPES + index(xh, src, z, core)
                    doc = docs[src][:, :1]
                    ok = (key_pos <= q_pos) & (key_pos >= doc)
                    allowed.extend([ok] * GROUP)
                parts = [
                    jnp.where(ok, scores[n * TILE : (n + 1) * TILE], LOW)
                    for n, ok in enumerate(allowed)
                ]
                scores = jnp.concatenate(parts, axis=0)
            before = top[:, :1]
            now = jnp.maximum(before, jnp.max(scores, axis=1, keepdims=True))
            weights = jnp.exp2(scores - now)
            shrink = jnp.exp2(before - now)
            top[...] = jnp.broadcast_to(now, top.shape)
            total[...] = total[...] * shrink + jnp.sum(weights, axis=1, keepdims=True)
            acc[...] = acc[...] * shrink + jnp.dot(
                weights.astype(jnp.bfloat16), values, preferred_element_type=jnp.float32
            )

        def one(j, _):
            needs = (j == i) | (j * KEYS < high_doc)

            @pl.when(needs)
            def _():
                step(j, True)

            @pl.when(jnp.logical_not(needs))
            def _():
                step(j, False)

            return 0

        lax.fori_loop(low_doc // KEYS, i + 1, one, 0)
        context = (acc[...] / total[...]).astype(jnp.bfloat16)
        for src in range(NY):
            for r in range(GROUP):
                at = (src * GROUP + r) * TILE
                out_ref[src, rows, pl.ds(r * HD, HD)] = context[at : at + TILE]


def attend(kv, q, doc):
    vmem = pl.BlockSpec(memory_space=pltpu.VMEM)
    return pl.pallas_call(
        attend_kernel,
        out_shape=jax.ShapeDtypeStruct((NY, TOK, GROUP * HD), jnp.bfloat16),
        in_specs=[pl.BlockSpec(memory_space=pl.ANY), vmem, vmem],
        out_specs=vmem,
        scratch_shapes=[
            pltpu.VMEM((BLOCKS, STRIPES, TILE, HD), jnp.bfloat16),
            pltpu.VMEM((BLOCKS, STRIPES, TILE, HD), jnp.bfloat16),
            pltpu.VMEM((ROWS, HD), jnp.bfloat16),
            pltpu.VMEM((ROWS, HD), jnp.float32),
            pltpu.VMEM((ROWS, HD), jnp.float32),
            pltpu.VMEM((ROWS, HD), jnp.float32),
            pltpu.SemaphoreType.DMA((2, BLOCKS)),
        ],
        compiler_params=pltpu.CompilerParams(vmem_limit_bytes=48 * 2**20),
    )(kv, q, doc)


def project_kernel(ctx, w, out_ref, cbuf, wbuf, acc, send, recv, wsem, local):
    xh, y, z, core, head = place()
    ypeer = [index(xh, (y + d) % NY, z, core) for d in range(NY)]
    others = [(ypeer[d], 1 - head) for d in range(NY)] + [(ypeer[d], head) for d in (1, 2, 3)]
    barrier = enter(others)
    order = [(head, (y + d) % NY) for d in range(NY)] + [(1 - head, (y + d) % NY) for d in range(NY)]
    fetches = []
    for n, (hh, p) in enumerate(order):
        rows = pl.ds(pl.multiple_of(hh * 1024 + p % 2 * 512, 512), 512)
        fetch = pltpu.make_async_copy(w.at[p // 2, rows], wbuf.at[n], wsem.at[n])
        fetches.append(fetch)
    mine = pltpu.make_async_copy(ctx.at[y], cbuf.at[head * 4 + y], local)
    mine.start()
    pl.semaphore_wait(barrier, len(others))
    started = []
    for hh, ds in ((1 - head, (2, 1, 3, 0)), (head, (2, 1, 3))):
        for d in ds:
            copy = pltpu.make_async_remote_copy(
                src_ref=ctx.at[(y + d) % NY],
                dst_ref=cbuf.at[head * 4 + y],
                send_sem=send.at[len(started)],
                recv_sem=recv.at[head * 4 + y],
                device_id=(ypeer[d], hh),
                device_id_type=MESH,
            )
            copy.start()
            started.append(copy)
    for fetch in fetches:
        fetch.start()
    acc[...] = jnp.zeros_like(acc)
    for n, (hh, p) in enumerate(order):
        at = hh * 4 + p
        fetches[n].wait()
        if n == 0:
            mine.wait()
        else:
            pltpu.make_async_remote_copy(
                src_ref=cbuf.at[at], dst_ref=cbuf.at[at], send_sem=send.at[0], recv_sem=recv.at[at],
                device_id=others[0], device_id_type=MESH,
            ).wait_recv()

        def tile(b, _):
            cols = pl.ds(pl.multiple_of(b * 512, 512), 512)
            acc[p // 2, :, cols] += jnp.dot(
                cbuf[at], wbuf[n, :, cols], preferred_element_type=jnp.float32
            )
            return 0

        lax.fori_loop(0, 4, tile, 0)
    out_ref[...] = acc[...].astype(jnp.bfloat16)
    for copy in started:
        copy.wait_send()


def project(ctx, w):
    hbm = pl.BlockSpec(memory_space=pl.ANY)
    dma = pltpu.SemaphoreType.DMA
    width = w.shape[2]
    return pl.pallas_call(
        project_kernel,
        out_shape=jax.ShapeDtypeStruct((2, TOK, width), jnp.bfloat16),
        in_specs=[hbm, hbm],
        out_specs=pl.BlockSpec(memory_space=pltpu.VMEM),
        scratch_shapes=[
            pltpu.VMEM((8, TOK, GROUP * HD), jnp.bfloat16),
            pltpu.VMEM((8, GROUP * HD, width), jnp.bfloat16),
            pltpu.VMEM((2, TOK, width), jnp.float32),
            dma((7,)),
            dma((8,)),
            dma((8,)),
            dma,
        ],
        compiler_params=pltpu.CompilerParams(
            collective_id=1, has_side_effects=True, vmem_limit_bytes=48 * 2**20
        ),
    )(ctx, w)


def local(queries, keys, values, doc_start, out_weight):
    freq = np.power(500000.0, -np.arange(HD // 2) * 2.0 / HD).astype(np.float32)
    freq = jnp.asarray(np.concatenate([freq, freq])[None, :])
    doc = jnp.broadcast_to(doc_start[:, None], (TOK, HD))
    kv, q, docs = gather(freq, queries, keys, values, doc)
    context = attend(kv, q, docs)
    return project(context, out_weight)


def solution(mesh):
    return jax.shard_map(
        local,
        mesh=mesh,
        in_specs=(
            P(None, "ctx", "head"),
            P(None, "ctx", "head"),
            P(None, "ctx", "head"),
            P("ctx"),
            P(None, None, "head"),
        ),
        out_specs=P(None, "ctx", "head"),
        check_vma=False,
    )
```

```python
import functools

import jax
import jax.numpy as jnp
import numpy as np
from jax import lax
from jax.experimental import pallas as pl
from jax.experimental.pallas import tpu as pltpu
from jax.sharding import PartitionSpec as P

MESH = pl.DeviceIdType.MESH
HD = 128
NY, NZ = 4, 4
TOK = 160
STRIPES = 64
GROUP = 4
WIDE = GROUP * HD
TILE = 16
BLOCKS = TOK // TILE
KEYS = TILE * STRIPES
ROWS = NY * GROUP * TILE
CHUNKS = 5
CT = TOK // CHUNKS
UNIT = 256
UNITS = KEYS // UNIT
LEAD = 3
LAST = 8320
LOW = -1e30
BIG = 2.0**40
SCALE = HD**-0.5 * 1.4426950408889634
SUMS = 16


def index(xh, y, z, core):
    return ((xh * NY + y) * NZ + z) * 2 + core


def rotated(x, cosine, sine):
    x = x.astype(jnp.float32)
    return (x * cosine + pltpu.roll(x, 64, 1) * sine).astype(jnp.bfloat16)


def first_key_block(i):
    return i // (LAST // KEYS + 1) * (LAST // KEYS)


def kernel(
    freq_ref, doc_ref, q_ref, k_ref, v_ref, w_ref, out_ref,
    kv, stage, qst, qall, docs, tables, dcol, kaug, causal, qbuf, vt,
    scores, tops, acc, ctx, cbuf, wbuf,
    ysend, yrecv, qsend, qrecv, dsend, drecv, zsend, zrecv, osend, orecv,
    bsend, brecv, csend, crecv, wsem,
):
    c_at = lax.axis_index("ctx")
    head = lax.axis_index("head")
    xh, y, z, core = c_at // 32, (c_at // 8) % NY, (c_at // 2) % NZ, c_at % 2
    xp = 1 - xh
    zup, zdown = (z + 1) % NZ, (z + 3) % NZ
    zfar = (z + 2) % NZ
    ys = [(y + d) % NY for d in range(NY)]
    peers = [(index(xh, ys[d], z, core), head) for d in range(NY)]
    across = [(index(xp, ys[d], z, core), head) for d in range(NY)]
    mirror = [(index(xh, ys[d], z, core), 1 - head) for d in range(NY)]
    above = (index(xh, y, zup, core), head)
    below = (index(xh, y, zdown, core), head)
    sibling = (index(xh, y, z, 1 - core), head)
    partners = peers[1:] + across + mirror + [above, below, sibling]

    def remote(src, dst, send, recv, device):
        return pltpu.make_async_remote_copy(
            src_ref=src, dst_ref=dst, send_sem=send, recv_sem=recv,
            device_id=device, device_id_type=MESH,
        )

    def arrived(ref, sem):
        remote(ref, ref, wsem.at[0], sem, sibling).wait_recv()

    def group(c, zz, cc, low=0, size=8):
        return kv.at[c, pl.ds((cc * NZ + zz) * 8 + low, size)]

    slot = (core * NZ + z) * 8 + xh * NY + y

    def chunk(c):
        return pl.ds(pl.multiple_of(c * CT, CT), CT)

    def key_copies(c):
        made = []
        for n, (d, device) in enumerate(
            [(0, across[0])] + [(d, t[d]) for d in (2, 1, 3) for t in (peers, across)]
        ):
            made.append(
                remote(stage.at[c, ys[d]], kv.at[c, slot], ysend.at[c, n], yrecv.at[c], device)
            )
        return made

    def query_copies(c):
        return [
            remote(
                qst.at[ys[d], chunk(c)], qall.at[y, chunk(c)], qsend.at[c, d - 1], qrecv.at[c],
                peers[d],
            )
            for d in (2, 1, 3)
        ]

    def doc_copies():
        return [
            remote(doc_ref, docs.at[y], dsend.at[d - 1], drecv.at[0], peers[d]) for d in (1, 2, 3)
        ]

    def near_copies(c):
        own = group(c, z, core)
        return [
            remote(own, own, zsend.at[c, 0], zrecv.at[c, 0], above),
            remote(own, own, zsend.at[c, 1], zrecv.at[c, 1], below),
        ]

    def far_copies(c):
        up, down = group(c, zdown, core, 0, 4), group(c, zup, core, 4, 4)
        return [
            remote(up, up, osend.at[c, 0], orecv.at[c, 0], above),
            remote(down, down, osend.at[c, 1], orecv.at[c, 1], below),
        ]

    def sibling_copies(c, low=0, high=4):
        made = []
        for n, zz in list(enumerate((z, zdown, zup, zfar)))[low:high]:
            ref = group(c, zz, core)
            made.append(remote(ref, ref, bsend.at[c, n], brecv.at[c, n], sibling))
        return made

    def context_copies(c):
        made = []
        for n, (d, device) in enumerate(
            [(d, mirror[d]) for d in (2, 1, 3, 0)] + [(d, peers[d]) for d in (2, 1, 3)]
        ):
            made.append(
                remote(
                    ctx.at[ys[d], chunk(c)], cbuf.at[head * 4 + y, chunk(c)],
                    csend.at[c, n], crecv.at[head * 4 + y], device,
                )
            )
        return made

    def start(copies):
        for copy in copies:
            copy.start()

    barrier = pltpu.get_barrier_semaphore()
    for device in partners:
        pl.semaphore_signal(barrier, inc=1, device_id=device, device_id_type=MESH)

    positions = lax.broadcasted_iota(jnp.int32, (TOK, HD), 0) * STRIPES + c_at
    angles = positions.astype(jnp.float32) * freq_ref[...]
    lane = lax.broadcasted_iota(jnp.int32, (TOK, HD), 1)
    sine = jnp.sin(angles)
    tables[0] = jnp.cos(angles)
    tables[1] = jnp.where(lane < HD // 2, -sine, sine)
    for p in range(4):
        cols = pl.ds(p % 2 * HD, HD)
        turned = rotated(k_ref[p // 2, :, cols], tables[0], tables[1])
        held = v_ref[p // 2, :, cols]
        for c in range(CHUNKS):
            stage[c, p, 0] = turned[c * CT : (c + 1) * CT]
            stage[c, p, 1] = held[c * CT : (c + 1) * CT]
    pl.semaphore_wait(barrier, len(partners))

    def send_keys(c):
        start(key_copies(c))
        pltpu.make_async_copy(stage.at[c, y], kv.at[c, slot], yrecv.at[c]).start()

    def send_queries(c):
        start(query_copies(c))
        pltpu.make_async_copy(qst.at[y, chunk(c)], qall.at[y, chunk(c)], qrecv.at[c]).start()

    send_keys(0)
    start(doc_copies())
    pltpu.make_async_copy(doc_ref, docs.at[y], drecv.at[0]).start()
    send_keys(1)
    for p in range(4):
        for r in range(GROUP):
            cols = pl.ds((p % 2 * GROUP + r) * HD, HD)
            qst[p, :, pl.ds(r * HD, HD)] = rotated(q_ref[p // 2, :, cols], tables[0], tables[1])
    send_queries(0)
    for c in range(2, CHUNKS):
        send_keys(c)
        send_queries(c - 1)
    send_queries(CHUNKS - 1)
    weights_in = [
        pltpu.make_async_copy(w_ref.at[m], wbuf.at[m], wsem.at[1 + m]) for m in range(2)
    ]
    start(weights_in)

    def near(c):
        arrived(group(c, z, core), yrecv.at[c])
        start(near_copies(c))
        start(sibling_copies(c, 0, 1))

    def far(c):
        arrived(group(c, zdown, core), zrecv.at[c, 0])
        arrived(group(c, zup, core), zrecv.at[c, 1])
        start(far_copies(c))
        start(sibling_copies(c, 1, 3))

    def whole(c):
        arrived(group(c, zfar, core, 0, 4), orecv.at[c, 0])
        arrived(group(c, zfar, core, 4, 4), orecv.at[c, 1])
        start(sibling_copies(c, 3, 4))

    def other(c):
        for n, zz in enumerate((z, zdown, zup, zfar)):
            arrived(group(c, zz, 1 - core), brecv.at[c, n])

    near(0)

    row = lax.broadcasted_iota(jnp.int32, (KEYS, HD), 0)
    col = lax.broadcasted_iota(jnp.int32, (KEYS, HD), 1)
    s = row // TILE
    key_at = (row % TILE) * STRIPES + (s % 8 * NZ + s // 8 % NZ) * 2 + s // 32
    kind = col - 64
    query_at = (kind % TILE) * STRIPES + index(xh, kind // TILE, z, core)
    causal[0] = jnp.zeros((KEYS, HD), jnp.bfloat16)
    causal[1] = jnp.where((kind >= 0) & (key_at > query_at), 1.0, 0.0).astype(jnp.bfloat16)
    vt[:, HD:, :] = jnp.ones((BLOCKS, SUMS, KEYS), jnp.bfloat16)
    qbuf[BLOCKS] = jnp.zeros((ROWS, 2 * HD), jnp.bfloat16)

    near(1)

    arrived(docs, drecv.at[0])
    seen = docs[...].astype(jnp.float32)

    def highest(values):
        return jnp.max(jnp.max(values, axis=(0, 1)).reshape(1, -1), axis=1, keepdims=True)

    cut_a = highest(seen)
    cut_b = highest(jnp.where(seen < cut_a, seen, -1.0))
    cut_c = highest(jnp.where(seen < cut_b, seen, -1.0))
    one_lane = lax.broadcasted_iota(jnp.int32, (1, HD), 1)
    cuts = jnp.where(
        one_lane == 0, cut_a, jnp.where(one_lane == 1, cut_b, jnp.where(one_lane == 2, cut_c, -5.0))
    )
    for src in range(NY):
        line = seen[src]
        dcol[src, :HD] = jnp.broadcast_to(line[:1, :HD], (HD, HD)).T
        dcol[src, HD:] = jnp.broadcast_to(line[:1, HD:], (HD, HD)).T[: TOK - HD]
    key_pos = key_at.astype(jnp.float32)

    def key_mask(j, _):
        base = (j * KEYS).astype(jnp.float32)
        kaug[j] = jnp.where(key_pos + base < cuts, 1.0, 0.0).astype(jnp.bfloat16)
        return 0

    lax.fori_loop(0, BLOCKS, key_mask, 0)

    def tile(i):
        return pl.ds(pl.multiple_of(i * TILE, TILE), TILE)

    small_lane = lax.broadcasted_iota(jnp.int32, (TILE, HD), 1)
    small_row = lax.broadcasted_iota(jnp.int32, (TILE, HD), 0)

    def take_queries(c):
        arrived(qall.at[:, chunk(c)], qrecv.at[c])

        def one(n, _):
            i = c * 2 + n
            for src in range(NY):
                hit = (dcol[src, tile(i), :] == cuts) | (small_lane == 64 + src * TILE + small_row)
                mask = jnp.where(hit, -BIG, 0.0).astype(jnp.bfloat16)
                for r in range(GROUP):
                    at = pl.ds((src * GROUP + r) * TILE, TILE)
                    qbuf[i, at, :HD] = qall[src, tile(i), pl.ds(r * HD, HD)]
                    qbuf[i, at, HD:] = mask
            return 0

        lax.fori_loop(0, 2, one, 0)

    far(0)
    take_queries(0)
    whole(0)
    near(2)
    other(0)

    def score(i, j, h, first):
        slots = pl.ds(h * UNIT // TILE, UNIT // TILE)
        at = pl.ds(h * UNIT, UNIT)
        rows = pl.ds(pl.multiple_of(j % 2 * TILE, TILE), TILE)
        keys = kv[j // 2, slots, 0, rows, :].reshape(UNIT, HD)
        mask = kaug[j, at, :] + causal[(j + 1) // (i + 1), at, :]
        found = lax.dot_general(
            jnp.concatenate([keys, mask], axis=1), qbuf[i], (((1,), (1,)), ((), ())),
            preferred_element_type=jnp.float32,
        )
        scores[h] = found
        before = jnp.full((1, ROWS), LOW, jnp.float32) if first else tops[(h - 1) % UNITS, :1, :]
        now = jnp.maximum(before, jnp.max(found, axis=0, keepdims=True))
        tops[h, :1, :] = now
        tops[h, 1:2, :] = jnp.exp2((before - now) * SCALE)

    def absorb(j, h):
        top = tops[h, :1, :] * SCALE
        weights = jnp.exp2(scores[h] * SCALE - top).astype(jnp.bfloat16)
        acc[...] = acc[...] * tops[h, 1:2, :] + jnp.dot(
            vt[j, :, pl.ds(h * UNIT, UNIT)], weights, preferred_element_type=jnp.float32
        )

    acc[...] = jnp.zeros_like(acc)
    for h in range(LEAD):
        score(0, 0, h, h == 0)

    def block(i):
        def steps(j, next_i, next_j, last):
            for h in range(UNITS):
                if h + LEAD < UNITS:
                    score(i, j, h + LEAD, False)
                else:
                    score(next_i, next_j, h + LEAD - UNITS, last and h + LEAD == UNITS)
                absorb(j, h)

        def one(j, _):
            steps(j, i, j + 1, False)
            return 0

        lax.fori_loop(first_key_block(i), i, one, 0)
        steps(i, i + 1, first_key_block(i + 1) % BLOCKS, True)
        done = (acc[:HD, :] / acc[HD : HD + 1, :]).T.astype(jnp.bfloat16)
        acc[...] = jnp.zeros_like(acc)
        for src in range(NY):
            for r in range(GROUP):
                at = (src * GROUP + r) * TILE
                ctx[src, tile(i), pl.ds(r * HD, HD)] = done[at : at + TILE]

    def body(c, _):
        @pl.when(c < CHUNKS - 1)
        def _():
            take_queries(c + 1)

        def turn(n, _):
            j = c * 2 + n
            rows = pl.ds(pl.multiple_of(n * TILE, TILE), TILE)
            vt[j, :HD, :] = kv[c, :, 1, rows, :].reshape(KEYS, HD).T
            return 0

        lax.fori_loop(0, 2, turn, 0)
        block(c * 2)

        @pl.when(c < CHUNKS - 1)
        def _():
            far(c + 1)

        @pl.when(c < CHUNKS - 3)
        def _():
            near(c + 3)

        block(c * 2 + 1)
        start(context_copies(c))
        pltpu.make_async_copy(
            ctx.at[y, chunk(c)], cbuf.at[head * 4 + y, chunk(c)], crecv.at[head * 4 + y]
        ).start()

        @pl.when(c < CHUNKS - 1)
        def _():
            whole(c + 1)
            other(c + 1)

        return 0

    lax.fori_loop(0, CHUNKS, body, 0)

    for n in range(8):
        arrived(cbuf.at[n], crecv.at[n])
    for copy in weights_in:
        copy.wait()

    def project(n, _):
        m = n // 4
        cols = pl.ds(pl.multiple_of(n % 4 * 512, 512), 512)
        rows = jnp.concatenate([cbuf[hh * 4 + m * 2 + g] for hh in range(2) for g in range(2)], axis=1)
        out_ref[m, :, cols] = jnp.dot(
            rows, wbuf[m, :, cols], preferred_element_type=jnp.float32
        ).astype(jnp.bfloat16)
        return 0

    lax.fori_loop(0, 8, project, 0)

    for copy in doc_copies():
        copy.wait_send()

    def drain(c, _):
        for copy in (
            key_copies(c) + query_copies(c) + near_copies(c) + far_copies(c)
            + sibling_copies(c) + context_copies(c)
        ):
            copy.wait_send()
        return 0

    lax.fori_loop(0, CHUNKS, drain, 0)


def local(queries, keys, values, doc_start, out_weight):
    freq = np.power(500000.0, -np.arange(HD // 2) * 2.0 / HD).astype(np.float32)
    freq = jnp.asarray(np.concatenate([freq, freq])[None, :])
    doc = jnp.broadcast_to(jnp.pad(doc_start, (0, 256 - TOK))[None, :], (8, 256))
    width = out_weight.shape[2]
    vmem = pl.BlockSpec(memory_space=pltpu.VMEM)
    hbm = pl.BlockSpec(memory_space=pl.ANY)
    dma = pltpu.SemaphoreType.DMA
    b16, f32 = jnp.bfloat16, jnp.float32
    return pl.pallas_call(
        kernel,
        out_shape=jax.ShapeDtypeStruct((2, TOK, width), b16),
        in_specs=[vmem] * 5 + [hbm],
        out_specs=vmem,
        scratch_shapes=[
            pltpu.VMEM((CHUNKS, STRIPES, 2, CT, HD), b16),
            pltpu.VMEM((CHUNKS, 4, 2, CT, HD), b16),
            pltpu.VMEM((4, TOK, WIDE), b16),
            pltpu.VMEM((4, TOK, WIDE), b16),
            pltpu.VMEM((4, 8, 256), jnp.int32),
            pltpu.VMEM((2, TOK, HD), f32),
            pltpu.VMEM((4, TOK, HD), f32),
            pltpu.VMEM((BLOCKS, KEYS, HD), b16),
            pltpu.VMEM((2, KEYS, HD), b16),
            pltpu.VMEM((BLOCKS + 1, ROWS, 2 * HD), b16),
            pltpu.VMEM((BLOCKS, HD + SUMS, KEYS), b16),
            pltpu.VMEM((UNITS, UNIT, ROWS), f32),
            pltpu.VMEM((UNITS, 8, ROWS), f32),
            pltpu.VMEM((HD + SUMS, ROWS), f32),
            pltpu.VMEM((4, TOK, WIDE), b16),
            pltpu.VMEM((8, TOK, WIDE), b16),
            pltpu.VMEM((2, 2048, width), b16),
            dma((CHUNKS, 7)),
            dma((CHUNKS,)),
            dma((CHUNKS, 3)),
            dma((CHUNKS,)),
            dma((3,)),
            dma((1,)),
            dma((CHUNKS, 2)),
            dma((CHUNKS, 2)),
            dma((CHUNKS, 2)),
            dma((CHUNKS, 2)),
            dma((CHUNKS, 4)),
            dma((CHUNKS, 4)),
            dma((CHUNKS, 7)),
            dma((8,)),
            dma((3,)),
        ],
        compiler_params=pltpu.CompilerParams(
            collective_id=0, has_side_effects=True, vmem_limit_bytes=56 * 2**20
        ),
    )(freq, doc, queries, keys, values, out_weight)


def solution(mesh):
    return jax.shard_map(
        local,
        mesh=mesh,
        in_specs=(
            P(None, "ctx", "head"),
            P(None, "ctx", "head"),
            P(None, "ctx", "head"),
            P("ctx"),
            P(None, None, "head"),
        ),
        out_specs=P(None, "ctx", "head"),
        check_vma=False,
    )
```

```python
import functools

import jax
import jax.numpy as jnp
import numpy as np
from jax import lax
from jax.experimental import pallas as pl
from jax.experimental.pallas import tpu as pltpu
from jax.sharding import PartitionSpec as P

MESH = pl.DeviceIdType.MESH
HD = 128
NY, NZ = 4, 4
TOK = 160
STRIPES = 64
GROUP = 4
WIDE = GROUP * HD
TILE = 16
BLOCKS = TOK // TILE
KEYS = TILE * STRIPES
ROWS = NY * GROUP * TILE
CHUNKS = 5
CT = TOK // CHUNKS
HALF = KEYS // 2
BUFFERS = 5
EARLY = 8 * TILE
LOW = -1e30
BIG = 2.0**40
SCALE = HD**-0.5 * 1.4426950408889634
SUMS = 16


def index(xh, y, z, core):
    return ((xh * NY + y) * NZ + z) * 2 + core


def rotated(x, cosine, sine):
    x = x.astype(jnp.float32)
    return (x * cosine + pltpu.roll(x, 64, 1) * sine).astype(jnp.bfloat16)


def kernel(
    freq_hbm, doc_hbm, q_hbm, k_hbm, v_hbm, w_ref, out_ref,
    freq_ref, doc_ref, q_ref, k_ref, v_ref, own_doc, kv, stage, qst, qall, docs, tables, dcol, kaug, causal, qbuf, vt,
    scores, tops, highs, acc, ctx, cbuf, wbuf,
    ysend, yrecv, qsend, qrecv, dsend, drecv, zsend, zrecv, osend, orecv,
    bsend, brecv, csend, crecv, wsem, isem,
):
    c_at = lax.axis_index("ctx")
    head = lax.axis_index("head")
    xh, y, z, core = c_at // 32, (c_at // 8) % NY, (c_at // 2) % NZ, c_at % 2
    xp = 1 - xh
    zup, zdown = (z + 1) % NZ, (z + 3) % NZ
    ys = [(y + d) % NY for d in range(NY)]
    peers = [(index(xh, ys[d], z, core), head) for d in range(NY)]
    across = [(index(xp, ys[d], z, core), head) for d in range(NY)]
    mirror = [(index(xh, ys[d], z, core), 1 - head) for d in range(NY)]
    above = (index(xh, y, zup, core), head)
    below = (index(xh, y, zdown, core), head)
    sibling = (index(xh, y, z, 1 - core), head)
    partners = peers[1:] + across + mirror + [above, below, sibling]

    def remote(src, dst, send, recv, device):
        return pltpu.make_async_remote_copy(
            src_ref=src, dst_ref=dst, send_sem=send, recv_sem=recv,
            device_id=device, device_id_type=MESH,
        )

    def arrived(ref, sem):
        remote(ref, ref, wsem.at[0], sem, sibling).wait_recv()

    def group(c, r, cc, low=0, size=8):
        return kv.at[c, pl.ds(r * 16 + cc * 8 + low, size)]

    slot = xh * NY + y

    def tile(i):
        return pl.ds(pl.multiple_of(i * TILE, TILE), TILE)

    def chunk(c):
        return pl.ds(pl.multiple_of(c * CT, CT), CT)

    def key_copies(c):
        made = []
        for n, (d, device) in enumerate(
            [(0, across[0])] + [(d, t[d]) for d in (2, 1, 3) for t in (peers, across)]
        ):
            made.append(
                remote(stage.at[c, ys[d]], kv.at[c, slot], ysend.at[c, n], yrecv.at[c], device)
            )
        return made

    def query_copies(c):
        return [
            remote(
                qst.at[ys[d], chunk(c)], qall.at[y, chunk(c)], qsend.at[c, d - 1], qrecv.at[c],
                peers[d],
            )
            for d in (2, 1, 3)
        ]

    def doc_copies():
        return [
            remote(own_doc, docs.at[y], dsend.at[d - 1], drecv.at[0], peers[d]) for d in (1, 2, 3)
        ]

    def near_copies(c):
        own = group(c, 0, 0)
        return [
            remote(own, group(c, 1, 0), zsend.at[c, 0], zrecv.at[c, 0], above),
            remote(own, group(c, 2, 0), zsend.at[c, 1], zrecv.at[c, 1], below),
        ]

    def far_copy(c, n):
        src, dst = group(c, 1 + n, 0, 4 * n, 4), group(c, 3, 0, 4 * n, 4)
        return remote(src, dst, osend.at[c, n], orecv.at[c, n], (above, below)[n])

    def sibling_copy(c, r):
        return remote(group(c, r, 0), group(c, r, 1), bsend.at[c, r], brecv.at[c, r], sibling)

    def context_copies(i):
        made = []
        part = i // 8
        for n, (d, device) in enumerate(
            [(d, mirror[d]) for d in (2, 1, 3, 0)] + [(d, peers[d]) for d in (2, 1, 3)]
        ):
            made.append(
                remote(
                    ctx.at[ys[d], tile(i)], cbuf.at[head * 4 + y, tile(i)],
                    csend.at[i, n], crecv.at[head * 4 + y, part], device,
                )
            )
        return made

    def send_context(i):
        start(context_copies(i))
        pltpu.make_async_copy(
            ctx.at[y, tile(i)], cbuf.at[head * 4 + y, tile(i)], crecv.at[head * 4 + y, i // 8]
        ).start()

    def start(copies):
        for copy in copies:
            copy.start()

    inputs = [
        pltpu.make_async_copy(src, dst, isem.at[n])
        for n, (src, dst) in enumerate(
            (
                (freq_hbm, freq_ref), (doc_hbm, doc_ref), (k_hbm, k_ref), (v_hbm, v_ref),
                (q_hbm, q_ref),
            )
        )
    ]
    start(inputs)
    barrier = pltpu.get_barrier_semaphore()
    for device in partners:
        pl.semaphore_signal(barrier, inc=1, device_id=device, device_id_type=MESH)

    positions = lax.broadcasted_iota(jnp.int32, (TOK, HD), 0) * STRIPES + c_at
    inputs[0].wait()
    angles = positions.astype(jnp.float32) * freq_ref[...]
    lane = lax.broadcasted_iota(jnp.int32, (TOK, HD), 1)
    sine = jnp.sin(angles)
    tables[0] = jnp.cos(angles)
    tables[1] = jnp.where(lane < HD // 2, -sine, sine)
    inputs[1].wait()
    own_doc[:, HD:] = jnp.zeros((8, HD), jnp.int32)
    own_doc[:1, :TOK] = doc_ref[...].reshape(1, TOK)
    inputs[2].wait()
    inputs[3].wait()
    for p in range(4):
        cols = pl.ds(p % 2 * HD, HD)
        turned = rotated(k_ref[p // 2, :, cols], tables[0], tables[1])
        held = v_ref[p // 2, :, cols]
        for c in range(CHUNKS):
            stage[c, p, 0] = turned[c * CT : (c + 1) * CT]
            stage[c, p, 1] = held[c * CT : (c + 1) * CT]
    pl.semaphore_wait(barrier, len(partners))

    def send_keys(c):
        start(key_copies(c))
        pltpu.make_async_copy(stage.at[c, y], kv.at[c, slot], yrecv.at[c]).start()

    def send_queries(c):
        start(query_copies(c))
        pltpu.make_async_copy(qst.at[y, chunk(c)], qall.at[y, chunk(c)], qrecv.at[c]).start()

    def near(c):
        arrived(group(c, 0, 0), yrecv.at[c])
        start(near_copies(c))
        sibling_copy(c, 0).start()

    def far(c):
        for n in range(2):
            arrived(group(c, 1 + n, 0), zrecv.at[c, n])
            far_copy(c, n).start()
            sibling_copy(c, 1 + n).start()

    def whole(c):
        for n in range(2):
            arrived(group(c, 3, 0, 4 * n, 4), orecv.at[c, n])
        sibling_copy(c, 3).start()

    def half(c, n):
        for r in (2 * n, 2 * n + 1):
            arrived(group(c, r, 1), brecv.at[c, r])

    send_keys(0)
    start(doc_copies())
    pltpu.make_async_copy(own_doc, docs.at[y], drecv.at[0]).start()
    send_keys(1)
    inputs[4].wait()
    for p in range(4):
        for r in range(GROUP):
            cols = pl.ds((p % 2 * GROUP + r) * HD, HD)
            qst[p, :, pl.ds(r * HD, HD)] = rotated(q_ref[p // 2, :, cols], tables[0], tables[1])
    send_queries(0)
    weights_in = [
        pltpu.make_async_copy(w_ref.at[m], wbuf.at[m], wsem.at[1 + m]) for m in range(2)
    ]
    start(weights_in)
    near(0)
    send_keys(2)
    send_queries(1)
    send_queries(2)
    send_keys(3)

    row = lax.broadcasted_iota(jnp.int32, (KEYS, HD), 0)
    col = lax.broadcasted_iota(jnp.int32, (KEYS, HD), 1)
    at = row // TILE
    rel = at // 16
    key_z = (z + jnp.where(rel == 1, 3, jnp.where(rel == 2, 1, jnp.where(rel == 3, 2, 0)))) % NZ
    key_core = (core + at // 8 % 2) % 2
    key_at = (row % TILE) * STRIPES + (at % 8 * NZ + key_z) * 2 + key_core
    kind = col - 64
    query_at = (kind % TILE) * STRIPES + index(xh, kind // TILE, z, core)
    causal[...] = jnp.where((kind >= 0) & (key_at > query_at), 1.0, 0.0).astype(jnp.bfloat16)
    vt[:, :, HD:, :] = jnp.ones((BLOCKS, 2, SUMS, HALF), jnp.bfloat16)
    qbuf[BLOCKS] = jnp.zeros((ROWS, 2 * HD), jnp.bfloat16)

    near(1)

    arrived(docs, drecv.at[0])
    seen = docs[...].astype(jnp.float32)

    def highest(values):
        return jnp.max(jnp.max(values, axis=(0, 1)).reshape(1, -1), axis=1, keepdims=True)

    cut_a = highest(seen)
    cut_b = highest(jnp.where(seen < cut_a, seen, -1.0))
    cut_c = highest(jnp.where(seen < cut_b, seen, -1.0))
    one_lane = lax.broadcasted_iota(jnp.int32, (1, HD), 1)
    cuts = jnp.where(
        one_lane == 0, cut_a, jnp.where(one_lane == 1, cut_b, jnp.where(one_lane == 2, cut_c, -5.0))
    )
    for src in range(NY):
        line = seen[src]
        dcol[src, :HD] = jnp.broadcast_to(line[:1, :HD], (HD, HD)).T
        dcol[src, HD:] = jnp.broadcast_to(line[:1, HD:], (HD, HD)).T[: TOK - HD]
    key_pos = key_at.astype(jnp.float32)

    def key_mask(j, _):
        base = (j * KEYS).astype(jnp.float32)
        kaug[j] = jnp.where(key_pos + base < cuts, 1.0, 0.0).astype(jnp.bfloat16)
        return 0

    lax.fori_loop(0, BLOCKS, key_mask, 0)

    small_lane = lax.broadcasted_iota(jnp.int32, (TILE, HD), 1)
    small_row = lax.broadcasted_iota(jnp.int32, (TILE, HD), 0)

    def take_queries(c):
        arrived(qall.at[:, chunk(c)], qrecv.at[c])

        def one(n, _):
            i = c * 2 + n
            for src in range(NY):
                hit = (dcol[src, tile(i), :] == cuts) | (small_lane == 64 + src * TILE + small_row)
                mask = jnp.where(hit, -BIG, 0.0).astype(jnp.bfloat16)
                for r in range(GROUP):
                    at = pl.ds((src * GROUP + r) * TILE, TILE)
                    qbuf[i, at, :HD] = qall[src, tile(i), pl.ds(r * HD, HD)]
                    qbuf[i, at, HD:] = mask
            return 0

        lax.fori_loop(0, 2, one, 0)

    take_queries(0)
    far(0)
    near(2)
    send_queries(3)
    send_keys(4)
    send_queries(4)
    take_queries(1)
    take_queries(2)
    half(0, 0)

    def score(buffer, i, j, n, diagonal=False):
        at = pl.ds(pl.multiple_of(n * HALF, HALF), HALF)
        slots = pl.ds(n * 32, 32)
        rows = pl.ds(pl.multiple_of(j % 2 * TILE, TILE), TILE)
        keys = kv[j // 2, slots, 0, rows, :].reshape(HALF, HD)
        mask = kaug[j, at, :]
        if diagonal:
            mask = mask + causal[at, :]
        found = lax.dot_general(
            jnp.concatenate([keys, mask], axis=1), qbuf[i], (((1,), (1,)), ((), ())),
            preferred_element_type=jnp.float32,
        )
        scores[buffer] = found
        before = highs[i, :1, :]
        now = jnp.maximum(before, jnp.max(found, axis=0, keepdims=True))
        highs[i, :1, :] = now
        tops[buffer, :1, :] = now
        tops[buffer, 1:2, :] = jnp.exp2((before - now) * SCALE)

    def absorb(buffer, i, j, n):
        top = tops[buffer, :1, :] * SCALE
        weights = jnp.exp2(scores[buffer] * SCALE - top).astype(jnp.bfloat16)
        acc[i] = acc[i] * tops[buffer, 1:2, :] + jnp.dot(
            vt[j, n], weights, preferred_element_type=jnp.float32
        )

    def finish(i):
        done = (acc[i, :HD, :] / acc[i, HD : HD + 1, :]).T.astype(jnp.bfloat16)
        for src in range(NY):
            for r in range(GROUP):
                at = (src * GROUP + r) * TILE
                ctx[src, tile(i), pl.ds(r * HD, HD)] = done[at : at + TILE]
        send_context(i)

    def turn(c, n):
        for b in range(2):
            rows = pl.ds(b * TILE, TILE)
            vt[c * 2 + b, n, :HD, :] = kv[c, pl.ds(n * 32, 32), 1, rows, :].reshape(HALF, HD).T

    services = {
        (0, 1): [(take_queries, 3), (near, 3)],
        (0, 2): [(take_queries, 4), (far, 1)],
        (0, 3): [(whole, 0), (half, 0, 1)],
        (1, 0): [(near, 4)],
        (1, 1): [(far, 2)],
        (1, 2): [(whole, 1)],
        (1, 3): [(half, 1, 0)],
        (2, 1): [(far, 3)],
        (2, 2): [(half, 1, 1)],
        (3, 0): [(whole, 2)],
        (3, 2): [(half, 2, 0)],
        (4, 1): [(far, 4), (half, 2, 1)],
        (5, 0): [(whole, 3)],
        (5, 1): [(half, 3, 0)],
        (6, 0): [(half, 3, 1)],
        (7, 0): [(whole, 4), (half, 4, 0)],
    }

    def serve(t, it):
        for (tt, nn), work in services.items():

            @pl.when((t == tt) & (it == nn))
            def _(work=work):
                for act, *args in work:
                    act(*args)

    acc[...] = jnp.zeros_like(acc)
    highs[...] = jnp.full_like(highs, LOW)
    score(4, 0, 0, 0, True)
    score(0, 1, 0, 0)
    score(1, 1, 1, 0, True)

    def body(t, _):
        c, n = t // 2, t % 2
        even, odd = c * 2, c * 2 + 1
        next_even, next_n = (t + 1) // 2 * 2, (t + 1) % 2
        turn(c, n)
        score(2, even + 2, even, n)
        absorb(4, even, even, n)

        def rest(it, _):
            i = odd + it * 2
            serve(t, it)

            def four(after):
                score(3, i + 1, odd, n)
                absorb(0, i, even, n)
                after[0]()
                absorb(1, i, odd, n)
                after[1]()
                absorb(2, i + 1, even, n)
                after[2]()
                absorb(3, i + 1, odd, n)

            @pl.when(it < 3 - c)
            def _():
                four(
                    [
                        lambda: score(0, i + 2, even, n),
                        lambda: score(1, i + 2, odd, n),
                        lambda: score(2, i + 3, even, n),
                    ]
                )

            @pl.when(it == 3 - c)
            def _():
                four(
                    [
                        lambda: score(4, next_even, next_even, next_n, True),
                        lambda: score(0, next_even + 1, next_even, next_n),
                        lambda: score(1, next_even + 1, next_even + 1, next_n, True),
                    ]
                )

            @pl.when((it == 0) & (n == 1))
            def _():
                finish(even)
                finish(odd)

            return 0

        lax.fori_loop(0, 4 - c, rest, 0)
        return 0

    lax.fori_loop(0, 8, body, 0)
    turn(4, 0)
    half(4, 1)
    turn(4, 1)
    score(2, 8, 8, 1, True)
    absorb(4, 8, 8, 0)
    score(3, 9, 8, 1)
    absorb(0, 9, 8, 0)
    score(4, 9, 9, 1, True)
    absorb(1, 9, 9, 0)
    absorb(2, 8, 8, 1)
    finish(8)
    absorb(3, 9, 8, 1)
    absorb(4, 9, 9, 1)
    finish(9)

    for copy in weights_in:
        copy.wait()

    def project(first, size, part):
        for n in range(8):
            arrived(cbuf.at[n, pl.ds(first, size)], crecv.at[n, part])

        def one(n, _):
            m = n // 4
            cols = pl.ds(pl.multiple_of(n % 4 * 512, 512), 512)
            rows = jnp.concatenate(
                [cbuf[h * 4 + m * 2 + g, first : first + size] for h in range(2) for g in range(2)],
                axis=1,
            )
            out_ref[m, first : first + size, cols] = jnp.dot(
                rows, wbuf[m, :, cols], preferred_element_type=jnp.float32
            ).astype(jnp.bfloat16)
            return 0

        lax.fori_loop(0, 8, one, 0)

    project(0, EARLY, 0)
    project(EARLY, TOK - EARLY, 1)

    for copy in doc_copies():
        copy.wait_send()

    def drain(c, _):
        for copy in (
            key_copies(c) + query_copies(c) + near_copies(c) + [far_copy(c, 0), far_copy(c, 1)]
            + [sibling_copy(c, r) for r in range(4)]
            + context_copies(c * 2) + context_copies(c * 2 + 1)
        ):
            copy.wait_send()
        return 0

    lax.fori_loop(0, CHUNKS, drain, 0)


def local(queries, keys, values, doc_start, out_weight):
    freq = np.power(500000.0, -np.arange(HD // 2) * 2.0 / HD).astype(np.float32)
    freq = jnp.asarray(np.concatenate([freq, freq])[None, :])
    width = out_weight.shape[2]
    vmem = pl.BlockSpec(memory_space=pltpu.VMEM)
    hbm = pl.BlockSpec(memory_space=pltpu.HBM)
    dma = pltpu.SemaphoreType.DMA
    b16, f32 = jnp.bfloat16, jnp.float32
    return pl.pallas_call(
        kernel,
        out_shape=jax.ShapeDtypeStruct((2, TOK, width), b16),
        in_specs=[hbm] * 6,
        out_specs=vmem,
        scratch_shapes=[
            pltpu.VMEM(freq.shape, f32),
            pltpu.VMEM(doc_start.shape, jnp.int32),
            pltpu.VMEM(queries.shape, b16),
            pltpu.VMEM(keys.shape, b16),
            pltpu.VMEM(values.shape, b16),
            pltpu.VMEM((8, 256), jnp.int32),
            pltpu.VMEM((CHUNKS, STRIPES, 2, CT, HD), b16),
            pltpu.VMEM((CHUNKS, 4, 2, CT, HD), b16),
            pltpu.VMEM((4, TOK, WIDE), b16),
            pltpu.VMEM((4, TOK, WIDE), b16),
            pltpu.VMEM((4, 8, 256), jnp.int32),
            pltpu.VMEM((2, TOK, HD), f32),
            pltpu.VMEM((4, TOK, HD), f32),
            pltpu.VMEM((BLOCKS, KEYS, HD), b16),
            pltpu.VMEM((KEYS, HD), b16),
            pltpu.VMEM((BLOCKS + 1, ROWS, 2 * HD), b16),
            pltpu.VMEM((BLOCKS, 2, HD + SUMS, HALF), b16),
            pltpu.VMEM((BUFFERS, HALF, ROWS), f32),
            pltpu.VMEM((BUFFERS, 8, ROWS), f32),
            pltpu.VMEM((BLOCKS + 1, 8, ROWS), f32),
            pltpu.VMEM((BLOCKS, HD + SUMS, ROWS), f32),
            pltpu.VMEM((4, TOK, WIDE), b16),
            pltpu.VMEM((8, TOK, WIDE), b16),
            pltpu.VMEM((2, 2048, width), b16),
            dma((CHUNKS, 7)),
            dma((CHUNKS,)),
            dma((CHUNKS, 3)),
            dma((CHUNKS,)),
            dma((3,)),
            dma((1,)),
            dma((CHUNKS, 2)),
            dma((CHUNKS, 2)),
            dma((CHUNKS, 2)),
            dma((CHUNKS, 2)),
            dma((CHUNKS, 4)),
            dma((CHUNKS, 4)),
            dma((BLOCKS, 7)),
            dma((8, 2)),
            dma((3,)),
            dma((5,)),
        ],
        compiler_params=pltpu.CompilerParams(
            collective_id=0, has_side_effects=True, vmem_limit_bytes=44 * 2**20
        ),
    )(*(pltpu.with_memory_space_constraint(x, pltpu.HBM) for x in (freq, doc_start, queries, keys, values, out_weight)))


def solution(mesh):
    return jax.shard_map(
        local,
        mesh=mesh,
        in_specs=(
            P(None, "ctx", "head"),
            P(None, "ctx", "head"),
            P(None, "ctx", "head"),
            P("ctx"),
            P(None, None, "head"),
        ),
        out_specs=P(None, "ctx", "head"),
        check_vma=False,
    )
```

```python
import functools

import jax
import jax.numpy as jnp
import numpy as np
from jax import lax
from jax.experimental import pallas as pl
from jax.experimental.pallas import tpu as pltpu
from jax.sharding import PartitionSpec as P

MESH = pl.DeviceIdType.MESH
HD = 128
NY, NZ = 4, 4
TOK = 160
STRIPES = 64
GROUP = 4
WIDE = GROUP * HD
TILE = 16
BLOCKS = TOK // TILE
KEYS = TILE * STRIPES
ROWS = NY * GROUP * TILE
CHUNKS = 5
CT = TOK // CHUNKS
HALF = KEYS // 2
BUFFERS = 5
EARLY = 8 * TILE
LOW = -1e30
BIG = 2.0**40
SCALE = HD**-0.5 * 1.4426950408889634
SUMS = 16


def index(xh, y, z, core):
    return ((xh * NY + y) * NZ + z) * 2 + core


def rotated(x, cosine, sine):
    x = x.astype(jnp.float32)
    return (x * cosine + pltpu.roll(x, 64, 1) * sine).astype(jnp.bfloat16)


def kernel(
    freq_hbm, doc_hbm, q_hbm, k_hbm, v_hbm, w_ref, out_ref,
    freq_ref, doc_ref, q_ref, k_ref, v_ref, own_doc, kv, stage, qst, qall, docs, tables, dcol, kaug, causal, qbuf, vt,
    scores, tops, highs, acc, ctx, cbuf, wbuf,
    ysend, yrecv, qsend, qrecv, dsend, drecv, zsend, zrecv, osend, orecv,
    bsend, brecv, csend, crecv, wsem, isem,
):
    c_at = lax.axis_index("ctx")
    head = lax.axis_index("head")
    xh, y, z, core = c_at // 32, (c_at // 8) % NY, (c_at // 2) % NZ, c_at % 2
    xp = 1 - xh
    zup, zdown = (z + 1) % NZ, (z + 3) % NZ
    ys = [(y + d) % NY for d in range(NY)]
    peers = [(index(xh, ys[d], z, core), head) for d in range(NY)]
    across = [(index(xp, ys[d], z, core), head) for d in range(NY)]
    mirror = [(index(xh, ys[d], z, core), 1 - head) for d in range(NY)]
    above = (index(xh, y, zup, core), head)
    below = (index(xh, y, zdown, core), head)
    sibling = (index(xh, y, z, 1 - core), head)
    partners = peers[1:] + across + mirror + [above, below, sibling]

    def remote(src, dst, send, recv, device):
        return pltpu.make_async_remote_copy(
            src_ref=src, dst_ref=dst, send_sem=send, recv_sem=recv,
            device_id=device, device_id_type=MESH,
        )

    def arrived(ref, sem):
        remote(ref, ref, wsem.at[0], sem, sibling).wait_recv()

    def group(c, r, cc, low=0, size=8):
        return kv.at[c, pl.ds(r * 16 + cc * 8 + low, size)]

    slot = xh * NY + y

    def tile(i):
        return pl.ds(pl.multiple_of(i * TILE, TILE), TILE)

    def chunk(c):
        return pl.ds(pl.multiple_of(c * CT, CT), CT)

    def key_copies(c):
        made = []
        for n, (d, device) in enumerate(
            [(0, across[0])] + [(d, t[d]) for d in (2, 1, 3) for t in (peers, across)]
        ):
            made.append(
                remote(stage.at[c, ys[d]], kv.at[c, slot], ysend.at[c, n], yrecv.at[c], device)
            )
        return made

    def query_copies(c):
        return [
            remote(
                qst.at[ys[d], chunk(c)], qall.at[y, chunk(c)], qsend.at[c, d - 1], qrecv.at[c],
                peers[d],
            )
            for d in (2, 1, 3)
        ]

    def doc_copies():
        return [
            remote(own_doc, docs.at[y], dsend.at[d - 1], drecv.at[0], peers[d]) for d in (1, 2, 3)
        ]

    def near_copies(c):
        own = group(c, 0, 0)
        return [
            remote(own, group(c, 1, 0), zsend.at[c, 0], zrecv.at[c, 0], above),
            remote(own, group(c, 2, 0), zsend.at[c, 1], zrecv.at[c, 1], below),
        ]

    def far_copy(c, n):
        src, dst = group(c, 1 + n, 0, 4 * n, 4), group(c, 3, 0, 4 * n, 4)
        return remote(src, dst, osend.at[c, n], orecv.at[c, n], (above, below)[n])

    def sibling_copy(c, r):
        return remote(group(c, r, 0), group(c, r, 1), bsend.at[c, r], brecv.at[c, r], sibling)

    def context_copies(i):
        made = []
        part = i // 8
        for n, (d, device) in enumerate(
            [(d, mirror[d]) for d in (2, 1, 3, 0)] + [(d, peers[d]) for d in (2, 1, 3)]
        ):
            made.append(
                remote(
                    ctx.at[ys[d], tile(i)], cbuf.at[head * 4 + y, tile(i)],
                    csend.at[i, n], crecv.at[head * 4 + y, part], device,
                )
            )
        return made

    def send_context(i):
        start(context_copies(i))
        pltpu.make_async_copy(
            ctx.at[y, tile(i)], cbuf.at[head * 4 + y, tile(i)], crecv.at[head * 4 + y, i // 8]
        ).start()

    def start(copies):
        for copy in copies:
            copy.start()

    inputs = [
        pltpu.make_async_copy(src, dst, isem.at[n])
        for n, (src, dst) in enumerate(
            (
                (freq_hbm, freq_ref), (doc_hbm, doc_ref), (k_hbm, k_ref), (v_hbm, v_ref),
                (q_hbm, q_ref),
            )
        )
    ]
    start(inputs)
    barrier = pltpu.get_barrier_semaphore()
    for device in partners:
        pl.semaphore_signal(barrier, inc=1, device_id=device, device_id_type=MESH)

    positions = lax.broadcasted_iota(jnp.int32, (TOK, HD), 0) * STRIPES + c_at
    inputs[0].wait()
    angles = positions.astype(jnp.float32) * freq_ref[...]
    lane = lax.broadcasted_iota(jnp.int32, (TOK, HD), 1)
    sine = jnp.sin(angles)
    tables[0] = jnp.cos(angles)
    tables[1] = jnp.where(lane < HD // 2, -sine, sine)
    inputs[1].wait()
    own_doc[:, HD:] = jnp.zeros((8, HD), jnp.int32)
    own_doc[:1, :TOK] = doc_ref[...].reshape(1, TOK)
    inputs[2].wait()
    inputs[3].wait()
    for p in range(4):
        cols = pl.ds(p % 2 * HD, HD)
        turned = rotated(k_ref[p // 2, :, cols], tables[0], tables[1])
        held = v_ref[p // 2, :, cols]
        for c in range(CHUNKS):
            stage[c, p, 0] = turned[c * CT : (c + 1) * CT]
            stage[c, p, 1] = held[c * CT : (c + 1) * CT]
    pl.semaphore_wait(barrier, len(partners))

    def send_keys(c):
        start(key_copies(c))
        pltpu.make_async_copy(stage.at[c, y], kv.at[c, slot], yrecv.at[c]).start()

    def send_queries(c):
        start(query_copies(c))
        pltpu.make_async_copy(qst.at[y, chunk(c)], qall.at[y, chunk(c)], qrecv.at[c]).start()

    def near(c):
        arrived(group(c, 0, 0), yrecv.at[c])
        sibling_copy(c, 0).start()
        start(near_copies(c))

    def far(c):
        for n in range(2):
            arrived(group(c, 1 + n, 0), zrecv.at[c, n])
            sibling_copy(c, 1 + n).start()
            far_copy(c, n).start()

    def whole(c):
        for n in range(2):
            arrived(group(c, 3, 0, 4 * n, 4), orecv.at[c, n])
        sibling_copy(c, 3).start()

    def half(c, n):
        for r in (2 * n, 2 * n + 1):
            arrived(group(c, r, 1), brecv.at[c, r])

    send_keys(0)
    start(doc_copies())
    pltpu.make_async_copy(own_doc, docs.at[y], drecv.at[0]).start()
    send_keys(1)
    inputs[4].wait()
    for p in range(4):
        for r in range(GROUP):
            cols = pl.ds((p % 2 * GROUP + r) * HD, HD)
            qst[p, :, pl.ds(r * HD, HD)] = rotated(q_ref[p // 2, :, cols], tables[0], tables[1])
    send_queries(0)
    weights_in = [
        pltpu.make_async_copy(w_ref.at[m], wbuf.at[m], wsem.at[1 + m]) for m in range(2)
    ]
    start(weights_in)
    near(0)
    send_keys(2)
    send_queries(1)
    send_queries(2)
    send_keys(3)

    row = lax.broadcasted_iota(jnp.int32, (KEYS, HD), 0)
    col = lax.broadcasted_iota(jnp.int32, (KEYS, HD), 1)
    at = row // TILE
    rel = at // 16
    key_z = (z + jnp.where(rel == 1, 3, jnp.where(rel == 2, 1, jnp.where(rel == 3, 2, 0)))) % NZ
    key_core = (core + at // 8 % 2) % 2
    key_at = (row % TILE) * STRIPES + (at % 8 * NZ + key_z) * 2 + key_core
    kind = col - 64
    query_at = (kind % TILE) * STRIPES + index(xh, kind // TILE, z, core)
    causal[...] = jnp.where((kind >= 0) & (key_at > query_at), 1.0, 0.0).astype(jnp.bfloat16)
    vt[:, :, HD:, :] = jnp.ones((BLOCKS, 2, SUMS, HALF), jnp.bfloat16)
    qbuf[BLOCKS] = jnp.zeros((ROWS, 2 * HD), jnp.bfloat16)

    near(1)

    arrived(docs, drecv.at[0])
    seen = docs[...].astype(jnp.float32)

    def highest(values):
        return jnp.max(jnp.max(values, axis=(0, 1)).reshape(1, -1), axis=1, keepdims=True)

    cut_a = highest(seen)
    cut_b = highest(jnp.where(seen < cut_a, seen, -1.0))
    cut_c = highest(jnp.where(seen < cut_b, seen, -1.0))
    one_lane = lax.broadcasted_iota(jnp.int32, (1, HD), 1)
    cuts = jnp.where(
        one_lane == 0, cut_a, jnp.where(one_lane == 1, cut_b, jnp.where(one_lane == 2, cut_c, -5.0))
    )
    for src in range(NY):
        line = seen[src]
        dcol[src, :HD] = jnp.broadcast_to(line[:1, :HD], (HD, HD)).T
        dcol[src, HD:] = jnp.broadcast_to(line[:1, HD:], (HD, HD)).T[: TOK - HD]
    key_pos = key_at.astype(jnp.float32)

    def key_mask(j, _):
        base = (j * KEYS).astype(jnp.float32)
        kaug[j] = jnp.where(key_pos + base < cuts, 1.0, 0.0).astype(jnp.bfloat16)
        return 0

    lax.fori_loop(0, BLOCKS, key_mask, 0)

    small_lane = lax.broadcasted_iota(jnp.int32, (TILE, HD), 1)
    small_row = lax.broadcasted_iota(jnp.int32, (TILE, HD), 0)

    def take_queries(c):
        arrived(qall.at[:, chunk(c)], qrecv.at[c])

        def one(n, _):
            i = c * 2 + n
            for src in range(NY):
                hit = (dcol[src, tile(i), :] == cuts) | (small_lane == 64 + src * TILE + small_row)
                mask = jnp.where(hit, -BIG, 0.0).astype(jnp.bfloat16)
                for r in range(GROUP):
                    at = pl.ds((src * GROUP + r) * TILE, TILE)
                    qbuf[i, at, :HD] = qall[src, tile(i), pl.ds(r * HD, HD)]
                    qbuf[i, at, HD:] = mask
            return 0

        lax.fori_loop(0, 2, one, 0)

    take_queries(0)
    far(0)
    near(2)
    send_queries(3)
    send_keys(4)
    send_queries(4)
    take_queries(1)
    take_queries(2)
    half(0, 0)

    def score(buffer, i, j, n, diagonal=False):
        at = pl.ds(pl.multiple_of(n * HALF, HALF), HALF)
        slots = pl.ds(n * 32, 32)
        rows = pl.ds(pl.multiple_of(j % 2 * TILE, TILE), TILE)
        keys = kv[j // 2, slots, 0, rows, :].reshape(HALF, HD)
        mask = kaug[j, at, :]
        if diagonal:
            mask = mask + causal[at, :]
        found = lax.dot_general(
            jnp.concatenate([keys, mask], axis=1), qbuf[i], (((1,), (1,)), ((), ())),
            preferred_element_type=jnp.float32,
        )
        scores[buffer] = found
        before = highs[i, :1, :]
        now = jnp.maximum(before, jnp.max(found, axis=0, keepdims=True))
        highs[i, :1, :] = now
        tops[buffer, :1, :] = now
        tops[buffer, 1:2, :] = jnp.exp2((before - now) * SCALE)

    def absorb(buffer, i, j, n):
        top = tops[buffer, :1, :] * SCALE
        weights = jnp.exp2(scores[buffer] * SCALE - top).astype(jnp.bfloat16)
        acc[i] = acc[i] * tops[buffer, 1:2, :] + jnp.dot(
            vt[j, n], weights, preferred_element_type=jnp.float32
        )

    def finish(i):
        done = (acc[i, :HD, :] / acc[i, HD : HD + 1, :]).T.astype(jnp.bfloat16)
        for src in range(NY):
            for r in range(GROUP):
                at = (src * GROUP + r) * TILE
                ctx[src, tile(i), pl.ds(r * HD, HD)] = done[at : at + TILE]
        send_context(i)

    def turn(c, n):
        for b in range(2):
            rows = pl.ds(b * TILE, TILE)
            vt[c * 2 + b, n, :HD, :] = kv[c, pl.ds(n * 32, 32), 1, rows, :].reshape(HALF, HD).T

    services = {
        (0, 1): [(take_queries, 3), (near, 3)],
        (0, 2): [(take_queries, 4), (far, 1)],
        (0, 3): [(whole, 0), (half, 0, 1)],
        (1, 0): [(near, 4)],
        (1, 1): [(far, 2)],
        (1, 2): [(whole, 1)],
        (1, 3): [(half, 1, 0)],
        (2, 1): [(far, 3)],
        (2, 2): [(half, 1, 1)],
        (3, 0): [(whole, 2)],
        (3, 2): [(half, 2, 0)],
        (4, 1): [(far, 4), (half, 2, 1)],
        (5, 0): [(whole, 3)],
        (5, 1): [(half, 3, 0)],
        (6, 0): [(half, 3, 1)],
        (7, 0): [(half, 4, 0)],
    }

    def serve(t, it):
        for (tt, nn), work in services.items():

            @pl.when((t == tt) & (it == nn))
            def _(work=work):
                for act, *args in work:
                    act(*args)

    acc[...] = jnp.zeros_like(acc)
    highs[...] = jnp.full_like(highs, LOW)
    score(4, 0, 0, 0, True)
    score(0, 1, 0, 0)
    score(1, 1, 1, 0, True)

    def body(t, _):
        c, n = t // 2, t % 2
        even, odd = c * 2, c * 2 + 1
        next_even, next_n = (t + 1) // 2 * 2, (t + 1) % 2
        turn(c, n)
        score(2, even + 2, even, n)
        absorb(4, even, even, n)

        def rest(it, _):
            i = odd + it * 2
            serve(t, it)

            def four(after):
                score(3, i + 1, odd, n)
                absorb(0, i, even, n)
                after[0]()
                absorb(1, i, odd, n)
                after[1]()
                absorb(2, i + 1, even, n)
                after[2]()
                absorb(3, i + 1, odd, n)

            @pl.when(it < 3 - c)
            def _():
                four(
                    [
                        lambda: score(0, i + 2, even, n),
                        lambda: score(1, i + 2, odd, n),
                        lambda: score(2, i + 3, even, n),
                    ]
                )

            @pl.when(it == 3 - c)
            def _():
                four(
                    [
                        lambda: score(4, next_even, next_even, next_n, True),
                        lambda: score(0, next_even + 1, next_even, next_n),
                        lambda: score(1, next_even + 1, next_even + 1, next_n, True),
                    ]
                )

            @pl.when((it == 0) & (n == 1))
            def _():
                finish(even)
                finish(odd)

            return 0

        lax.fori_loop(0, 4 - c, rest, 0)
        return 0

    lax.fori_loop(0, 8, body, 0)
    whole(4)
    turn(4, 0)
    absorb(4, 8, 8, 0)
    absorb(0, 9, 8, 0)
    absorb(1, 9, 9, 0)
    half(4, 1)
    turn(4, 1)
    score(2, 8, 8, 1, True)
    score(3, 9, 8, 1)
    score(4, 9, 9, 1, True)
    absorb(2, 8, 8, 1)
    finish(8)
    absorb(3, 9, 8, 1)
    absorb(4, 9, 9, 1)
    finish(9)

    for copy in weights_in:
        copy.wait()

    def project(first, size, part):
        for n in range(8):
            arrived(cbuf.at[n, pl.ds(first, size)], crecv.at[n, part])

        def one(n, _):
            m = n // 4
            cols = pl.ds(pl.multiple_of(n % 4 * 512, 512), 512)
            rows = jnp.concatenate(
                [cbuf[h * 4 + m * 2 + g, first : first + size] for h in range(2) for g in range(2)],
                axis=1,
            )
            out_ref[m, first : first + size, cols] = jnp.dot(
                rows, wbuf[m, :, cols], preferred_element_type=jnp.float32
            ).astype(jnp.bfloat16)
            return 0

        lax.fori_loop(0, 8, one, 0)

    project(0, EARLY, 0)
    project(EARLY, TOK - EARLY, 1)

    for copy in doc_copies():
        copy.wait_send()

    def drain(c, _):
        for copy in (
            key_copies(c) + query_copies(c) + near_copies(c) + [far_copy(c, 0), far_copy(c, 1)]
            + [sibling_copy(c, r) for r in range(4)]
            + context_copies(c * 2) + context_copies(c * 2 + 1)
        ):
            copy.wait_send()
        return 0

    lax.fori_loop(0, CHUNKS, drain, 0)


def local(queries, keys, values, doc_start, out_weight):
    freq = np.power(500000.0, -np.arange(HD // 2) * 2.0 / HD).astype(np.float32)
    freq = jnp.asarray(np.concatenate([freq, freq])[None, :])
    width = out_weight.shape[2]
    vmem = pl.BlockSpec(memory_space=pltpu.VMEM)
    hbm = pl.BlockSpec(memory_space=pltpu.HBM)
    dma = pltpu.SemaphoreType.DMA
    b16, f32 = jnp.bfloat16, jnp.float32
    return pl.pallas_call(
        kernel,
        out_shape=jax.ShapeDtypeStruct((2, TOK, width), b16),
        in_specs=[hbm] * 6,
        out_specs=vmem,
        scratch_shapes=[
            pltpu.VMEM(freq.shape, f32),
            pltpu.VMEM(doc_start.shape, jnp.int32),
            pltpu.VMEM(queries.shape, b16),
            pltpu.VMEM(keys.shape, b16),
            pltpu.VMEM(values.shape, b16),
            pltpu.VMEM((8, 256), jnp.int32),
            pltpu.VMEM((CHUNKS, STRIPES, 2, CT, HD), b16),
            pltpu.VMEM((CHUNKS, 4, 2, CT, HD), b16),
            pltpu.VMEM((4, TOK, WIDE), b16),
            pltpu.VMEM((4, TOK, WIDE), b16),
            pltpu.VMEM((4, 8, 256), jnp.int32),
            pltpu.VMEM((2, TOK, HD), f32),
            pltpu.VMEM((4, TOK, HD), f32),
            pltpu.VMEM((BLOCKS, KEYS, HD), b16),
            pltpu.VMEM((KEYS, HD), b16),
            pltpu.VMEM((BLOCKS + 1, ROWS, 2 * HD), b16),
            pltpu.VMEM((BLOCKS, 2, HD + SUMS, HALF), b16),
            pltpu.VMEM((BUFFERS, HALF, ROWS), f32),
            pltpu.VMEM((BUFFERS, 8, ROWS), f32),
            pltpu.VMEM((BLOCKS + 1, 8, ROWS), f32),
            pltpu.VMEM((BLOCKS, HD + SUMS, ROWS), f32),
            pltpu.VMEM((4, TOK, WIDE), b16),
            pltpu.VMEM((8, TOK, WIDE), b16),
            pltpu.VMEM((2, 2048, width), b16),
            dma((CHUNKS, 7)),
            dma((CHUNKS,)),
            dma((CHUNKS, 3)),
            dma((CHUNKS,)),
            dma((3,)),
            dma((1,)),
            dma((CHUNKS, 2)),
            dma((CHUNKS, 2)),
            dma((CHUNKS, 2)),
            dma((CHUNKS, 2)),
            dma((CHUNKS, 4)),
            dma((CHUNKS, 4)),
            dma((BLOCKS, 7)),
            dma((8, 2)),
            dma((3,)),
            dma((5,)),
        ],
        compiler_params=pltpu.CompilerParams(
            collective_id=0, has_side_effects=True, vmem_limit_bytes=44 * 2**20
        ),
    )(*(pltpu.with_memory_space_constraint(x, pltpu.HBM) for x in (freq, doc_start, queries, keys, values, out_weight)))


def solution(mesh):
    return jax.shard_map(
        local,
        mesh=mesh,
        in_specs=(
            P(None, "ctx", "head"),
            P(None, "ctx", "head"),
            P(None, "ctx", "head"),
            P("ctx"),
            P(None, None, "head"),
        ),
        out_specs=P(None, "ctx", "head"),
        check_vma=False,
    )
```

```python
import functools

import jax
import jax.numpy as jnp
import numpy as np
from jax import lax
from jax.experimental import pallas as pl
from jax.experimental.pallas import tpu as pltpu
from jax.sharding import PartitionSpec as P

MESH = pl.DeviceIdType.MESH
HD = 128
NY, NZ = 4, 4
TOK = 160
STRIPES = 64
GROUP = 4
WIDE = GROUP * HD
TILE = 16
BLOCKS = TOK // TILE
KEYS = TILE * STRIPES
ROWS = NY * GROUP * TILE
CHUNKS = 5
CT = TOK // CHUNKS
HALF = KEYS // 2
BUFFERS = 5
EARLY = 8 * TILE
LOW = -1e30
BIG = 2.0**40
SCALE = HD**-0.5 * 1.4426950408889634
SUMS = 16


def index(xh, y, z, core):
    return ((xh * NY + y) * NZ + z) * 2 + core


def rotated(x, cosine, sine):
    x = x.astype(jnp.float32)
    return (x * cosine + pltpu.roll(x, 64, 1) * sine).astype(jnp.bfloat16)


def kernel(
    freq_hbm, doc_hbm, q_hbm, k_hbm, v_hbm, w_ref, out_ref,
    freq_ref, doc_ref, q_ref, k_ref, v_ref, own_doc, kv, stage, qst, qall, docs, tables, dcol, kaug, causal, qbuf, vt,
    scores, tops, highs, acc, ctx, cbuf, wbuf,
    ysend, yrecv, qsend, qrecv, dsend, drecv, zsend, zrecv, osend, orecv,
    bsend, brecv, csend, crecv, wsem, isem,
):
    c_at = lax.axis_index("ctx")
    head = lax.axis_index("head")
    xh, y, z, core = c_at // 32, (c_at // 8) % NY, (c_at // 2) % NZ, c_at % 2
    xp = 1 - xh
    zup, zdown = (z + 1) % NZ, (z + 3) % NZ
    ys = [(y + d) % NY for d in range(NY)]
    peers = [(index(xh, ys[d], z, core), head) for d in range(NY)]
    across = [(index(xp, ys[d], z, core), head) for d in range(NY)]
    mirror = [(index(xh, ys[d], z, core), 1 - head) for d in range(NY)]
    above = (index(xh, y, zup, core), head)
    below = (index(xh, y, zdown, core), head)
    sibling = (index(xh, y, z, 1 - core), head)
    partners = peers[1:] + across + mirror + [above, below, sibling]

    def remote(src, dst, send, recv, device):
        return pltpu.make_async_remote_copy(
            src_ref=src, dst_ref=dst, send_sem=send, recv_sem=recv,
            device_id=device, device_id_type=MESH,
        )

    def arrived(ref, sem):
        remote(ref, ref, wsem.at[0], sem, sibling).wait_recv()

    def group(c, r, cc, low=0, size=8):
        return kv.at[c, pl.ds(r * 16 + cc * 8 + low, size)]

    slot = xh * NY + y

    def tile(i):
        return pl.ds(pl.multiple_of(i * TILE, TILE), TILE)

    def chunk(c):
        return pl.ds(pl.multiple_of(c * CT, CT), CT)

    def key_copies(c):
        made = []
        for n, (d, device) in enumerate(
            [(0, across[0])] + [(d, t[d]) for d in (2, 1, 3) for t in (peers, across)]
        ):
            made.append(
                remote(stage.at[c, ys[d]], kv.at[c, slot], ysend.at[c, n], yrecv.at[c], device)
            )
        return made

    def query_copies(c):
        return [
            remote(
                qst.at[ys[d], chunk(c)], qall.at[y, chunk(c)], qsend.at[c, d - 1], qrecv.at[c],
                peers[d],
            )
            for d in (2, 1, 3)
        ]

    def doc_copies():
        return [
            remote(own_doc, docs.at[y], dsend.at[d - 1], drecv.at[0], peers[d]) for d in (1, 2, 3)
        ]

    def near_copies(c):
        own = group(c, 0, 0)
        return [
            remote(own, group(c, 1, 0), zsend.at[c, 0], zrecv.at[c, 0], above),
            remote(own, group(c, 2, 0), zsend.at[c, 1], zrecv.at[c, 1], below),
        ]

    def far_copy(c, n):
        src, dst = group(c, 1 + n, 0, 4 * n, 4), group(c, 3, 0, 4 * n, 4)
        return remote(src, dst, osend.at[c, n], orecv.at[c, n], (above, below)[n])

    def sibling_copy(c, r):
        return remote(group(c, r, 0), group(c, r, 1), bsend.at[c, r], brecv.at[c, r], sibling)

    def context_copies(i):
        made = []
        part = i // 8
        for n, (d, device) in enumerate(
            [(d, mirror[d]) for d in (2, 1, 3, 0)] + [(d, peers[d]) for d in (2, 1, 3)]
        ):
            made.append(
                remote(
                    ctx.at[ys[d], tile(i)], cbuf.at[head * 4 + y, tile(i)],
                    csend.at[i, n], crecv.at[head * 4 + y, part], device,
                )
            )
        return made

    def send_context(i):
        start(context_copies(i))
        pltpu.make_async_copy(
            ctx.at[y, tile(i)], cbuf.at[head * 4 + y, tile(i)], crecv.at[head * 4 + y, i // 8]
        ).start()

    def start(copies):
        for copy in copies:
            copy.start()

    inputs = [
        pltpu.make_async_copy(src, dst, isem.at[n])
        for n, (src, dst) in enumerate(
            (
                (freq_hbm, freq_ref), (doc_hbm, doc_ref), (k_hbm, k_ref), (v_hbm, v_ref),
                (q_hbm, q_ref),
            )
        )
    ]
    start(inputs)
    barrier = pltpu.get_barrier_semaphore()
    for device in partners:
        pl.semaphore_signal(barrier, inc=1, device_id=device, device_id_type=MESH)

    positions = lax.broadcasted_iota(jnp.int32, (TOK, HD), 0) * STRIPES + c_at
    inputs[0].wait()
    angles = positions.astype(jnp.float32) * freq_ref[...]
    lane = lax.broadcasted_iota(jnp.int32, (TOK, HD), 1)
    sine = jnp.sin(angles)
    tables[0] = jnp.cos(angles)
    tables[1] = jnp.where(lane < HD // 2, -sine, sine)
    inputs[1].wait()
    own_doc[:, HD:] = jnp.zeros((8, HD), jnp.int32)
    own_doc[:1, :TOK] = doc_ref[...].reshape(1, TOK)
    inputs[2].wait()
    inputs[3].wait()
    for p in range(4):
        cols = pl.ds(p % 2 * HD, HD)
        turned = rotated(k_ref[p // 2, :, cols], tables[0], tables[1])
        held = v_ref[p // 2, :, cols]
        for c in range(CHUNKS):
            stage[c, p, 0] = turned[c * CT : (c + 1) * CT]
            stage[c, p, 1] = held[c * CT : (c + 1) * CT]
    pl.semaphore_wait(barrier, len(partners))

    def send_keys(c):
        start(key_copies(c))
        pltpu.make_async_copy(stage.at[c, y], kv.at[c, slot], yrecv.at[c]).start()

    def send_queries(c):
        start(query_copies(c))
        pltpu.make_async_copy(qst.at[y, chunk(c)], qall.at[y, chunk(c)], qrecv.at[c]).start()

    def near(c):
        arrived(group(c, 0, 0), yrecv.at[c])
        sibling_copy(c, 0).start()
        start(near_copies(c))

    def far(c):
        for n in range(2):
            arrived(group(c, 1 + n, 0), zrecv.at[c, n])
            sibling_copy(c, 1 + n).start()
            far_copy(c, n).start()

    def whole(c):
        for n in range(2):
            arrived(group(c, 3, 0, 4 * n, 4), orecv.at[c, n])
        sibling_copy(c, 3).start()

    def half(c, n):
        for r in (2 * n, 2 * n + 1):
            arrived(group(c, r, 1), brecv.at[c, r])

    send_keys(0)
    start(doc_copies())
    pltpu.make_async_copy(own_doc, docs.at[y], drecv.at[0]).start()
    send_keys(1)
    inputs[4].wait()
    for p in range(4):
        for r in range(GROUP):
            cols = pl.ds((p % 2 * GROUP + r) * HD, HD)
            qst[p, :, pl.ds(r * HD, HD)] = rotated(q_ref[p // 2, :, cols], tables[0], tables[1])
    send_queries(0)
    weights_in = [
        pltpu.make_async_copy(w_ref.at[m], wbuf.at[m], wsem.at[1 + m]) for m in range(2)
    ]
    start(weights_in)
    near(0)
    send_keys(2)
    send_queries(1)
    send_queries(2)
    send_keys(3)

    row = lax.broadcasted_iota(jnp.int32, (KEYS, HD), 0)
    col = lax.broadcasted_iota(jnp.int32, (KEYS, HD), 1)
    at = row // TILE
    rel = at // 16
    key_z = (z + jnp.where(rel == 1, 3, jnp.where(rel == 2, 1, jnp.where(rel == 3, 2, 0)))) % NZ
    key_core = (core + at // 8 % 2) % 2
    key_at = (row % TILE) * STRIPES + (at % 8 * NZ + key_z) * 2 + key_core
    kind = col - 64
    query_at = (kind % TILE) * STRIPES + index(xh, kind // TILE, z, core)
    causal[...] = jnp.where((kind >= 0) & (key_at > query_at), 1.0, 0.0).astype(jnp.bfloat16)
    vt[:, :, HD:, :] = jnp.ones((BLOCKS, 2, SUMS, HALF), jnp.bfloat16)
    qbuf[BLOCKS] = jnp.zeros((ROWS, 2 * HD), jnp.bfloat16)

    near(1)

    arrived(docs, drecv.at[0])
    seen = docs[...].astype(jnp.float32)

    def highest(values):
        return jnp.max(jnp.max(values, axis=(0, 1)).reshape(1, -1), axis=1, keepdims=True)

    cut_a = highest(seen)
    cut_b = highest(jnp.where(seen < cut_a, seen, -1.0))
    cut_c = highest(jnp.where(seen < cut_b, seen, -1.0))
    one_lane = lax.broadcasted_iota(jnp.int32, (1, HD), 1)
    cuts = jnp.where(
        one_lane == 0, cut_a, jnp.where(one_lane == 1, cut_b, jnp.where(one_lane == 2, cut_c, -5.0))
    )
    for src in range(NY):
        line = seen[src]
        dcol[src, :HD] = jnp.broadcast_to(line[:1, :HD], (HD, HD)).T
        dcol[src, HD:] = jnp.broadcast_to(line[:1, HD:], (HD, HD)).T[: TOK - HD]
    key_pos = key_at.astype(jnp.float32)

    def key_mask(j, _):
        base = (j * KEYS).astype(jnp.float32)
        kaug[j] = jnp.where(key_pos + base < cuts, 1.0, 0.0).astype(jnp.bfloat16)
        return 0

    lax.fori_loop(0, BLOCKS, key_mask, 0)

    small_lane = lax.broadcasted_iota(jnp.int32, (TILE, HD), 1)
    small_row = lax.broadcasted_iota(jnp.int32, (TILE, HD), 0)

    def take_queries(c):
        arrived(qall.at[:, chunk(c)], qrecv.at[c])

        def one(n, _):
            i = c * 2 + n
            for src in range(NY):
                hit = (dcol[src, tile(i), :] == cuts) | (small_lane == 64 + src * TILE + small_row)
                mask = jnp.where(hit, -BIG, 0.0).astype(jnp.bfloat16)
                for r in range(GROUP):
                    at = pl.ds((src * GROUP + r) * TILE, TILE)
                    qbuf[i, at, :HD] = qall[src, tile(i), pl.ds(r * HD, HD)]
                    qbuf[i, at, HD:] = mask
            return 0

        lax.fori_loop(0, 2, one, 0)

    take_queries(0)
    far(0)
    near(2)
    send_queries(3)
    send_keys(4)
    send_queries(4)
    take_queries(1)
    take_queries(2)
    half(0, 0)

    def score(buffer, i, j, n, diagonal=False):
        at = pl.ds(pl.multiple_of(n * HALF, HALF), HALF)
        slots = pl.ds(n * 32, 32)
        rows = pl.ds(pl.multiple_of(j % 2 * TILE, TILE), TILE)
        keys = kv[j // 2, slots, 0, rows, :].reshape(HALF, HD)
        mask = kaug[j, at, :]
        if diagonal:
            mask = mask + causal[at, :]
        found = lax.dot_general(
            jnp.concatenate([keys, mask], axis=1), qbuf[i], (((1,), (1,)), ((), ())),
            preferred_element_type=jnp.float32,
        )
        scores[buffer] = found
        before = highs[i, :1, :]
        now = jnp.maximum(before, jnp.max(found, axis=0, keepdims=True))
        highs[i, :1, :] = now
        tops[buffer, :1, :] = now
        tops[buffer, 1:2, :] = jnp.exp2((before - now) * SCALE)

    def absorb(buffer, i, j, n):
        top = tops[buffer, :1, :] * SCALE
        weights = jnp.exp2(scores[buffer] * SCALE - top).astype(jnp.bfloat16)
        acc[i] = acc[i] * tops[buffer, 1:2, :] + jnp.dot(
            vt[j, n], weights, preferred_element_type=jnp.float32
        )

    def finish(i):
        done = (acc[i, :HD, :] / acc[i, HD : HD + 1, :]).T.astype(jnp.bfloat16)
        for src in range(NY):
            for r in range(GROUP):
                at = (src * GROUP + r) * TILE
                ctx[src, tile(i), pl.ds(r * HD, HD)] = done[at : at + TILE]
        send_context(i)

    def turn(c, n):
        for b in range(2):
            rows = pl.ds(b * TILE, TILE)
            vt[c * 2 + b, n, :HD, :] = kv[c, pl.ds(n * 32, 32), 1, rows, :].reshape(HALF, HD).T

    services = {
        (0, 1): [(take_queries, 3), (near, 3)],
        (0, 2): [(take_queries, 4), (far, 1)],
        (0, 3): [(whole, 0), (half, 0, 1)],
        (1, 0): [(near, 4)],
        (1, 1): [(far, 2)],
        (1, 2): [(whole, 1)],
        (1, 3): [(half, 1, 0)],
        (2, 1): [(far, 3)],
        (2, 2): [(half, 1, 1)],
        (3, 0): [(whole, 2)],
        (3, 2): [(half, 2, 0)],
        (4, 1): [(far, 4), (half, 2, 1)],
        (5, 0): [(whole, 3)],
        (5, 1): [(half, 3, 0)],
        (6, 0): [(half, 3, 1)],
        (7, 0): [(half, 4, 0)],
    }

    def serve(t, it):
        for (tt, nn), work in services.items():

            @pl.when((t == tt) & (it == nn))
            def _(work=work):
                for act, *args in work:
                    act(*args)

    acc[...] = jnp.zeros_like(acc)
    highs[...] = jnp.full_like(highs, LOW)
    score(4, 0, 0, 0, True)
    score(0, 1, 0, 0)
    score(1, 1, 1, 0, True)

    def body(t, _):
        c, n = t // 2, t % 2
        even, odd = c * 2, c * 2 + 1
        next_even, next_n = (t + 1) // 2 * 2, (t + 1) % 2
        turn(c, n)
        score(2, even + 2, even, n)
        absorb(4, even, even, n)

        def rest(it, _):
            i = odd + it * 2
            serve(t, it)

            def four(after):
                score(3, i + 1, odd, n)
                absorb(0, i, even, n)
                after[0]()
                absorb(1, i, odd, n)
                after[1]()
                absorb(2, i + 1, even, n)
                after[2]()
                absorb(3, i + 1, odd, n)

            @pl.when(it < 3 - c)
            def _():
                four(
                    [
                        lambda: score(0, i + 2, even, n),
                        lambda: score(1, i + 2, odd, n),
                        lambda: score(2, i + 3, even, n),
                    ]
                )

            @pl.when(it == 3 - c)
            def _():
                four(
                    [
                        lambda: score(4, next_even, next_even, next_n, True),
                        lambda: score(0, next_even + 1, next_even, next_n),
                        lambda: score(1, next_even + 1, next_even + 1, next_n, True),
                    ]
                )

            @pl.when((it == 0) & (n == 1))
            def _():
                finish(even)
                finish(odd)

            return 0

        lax.fori_loop(0, 4 - c, rest, 0)
        return 0

    lax.fori_loop(0, 8, body, 0)
    whole(4)
    turn(4, 0)
    absorb(4, 8, 8, 0)
    absorb(0, 9, 8, 0)
    absorb(1, 9, 9, 0)
    half(4, 1)
    turn(4, 1)
    score(2, 8, 8, 1, True)
    score(3, 9, 8, 1)
    score(4, 9, 9, 1, True)
    absorb(2, 8, 8, 1)
    finish(8)
    absorb(3, 9, 8, 1)
    absorb(4, 9, 9, 1)
    finish(9)

    for copy in weights_in:
        copy.wait()

    def project(first, size, part):
        for n in range(8):
            arrived(cbuf.at[n, pl.ds(first, size)], crecv.at[n, part])

        def one(n, _):
            m = n // 2
            cols = pl.ds(pl.multiple_of(n % 2 * 1024, 1024), 1024)
            rows = jnp.concatenate(
                [cbuf[h * 4 + m * 2 + g, first : first + size] for h in range(2) for g in range(2)],
                axis=1,
            )
            out_ref[m, first : first + size, cols] = jnp.dot(
                rows, wbuf[m, :, cols], preferred_element_type=jnp.float32
            ).astype(jnp.bfloat16)
            return 0

        lax.fori_loop(0, 4, one, 0)

    project(0, EARLY, 0)
    project(EARLY, TOK - EARLY, 1)

    for copy in doc_copies():
        copy.wait_send()

    def drain(c, _):
        for copy in (
            key_copies(c) + query_copies(c) + near_copies(c) + [far_copy(c, 0), far_copy(c, 1)]
            + [sibling_copy(c, r) for r in range(4)]
            + context_copies(c * 2) + context_copies(c * 2 + 1)
        ):
            copy.wait_send()
        return 0

    lax.fori_loop(0, CHUNKS, drain, 0)


def local(queries, keys, values, doc_start, out_weight):
    freq = np.power(500000.0, -np.arange(HD // 2) * 2.0 / HD).astype(np.float32)
    freq = jnp.asarray(np.concatenate([freq, freq])[None, :])
    width = out_weight.shape[2]
    vmem = pl.BlockSpec(memory_space=pltpu.VMEM)
    hbm = pl.BlockSpec(memory_space=pltpu.HBM)
    dma = pltpu.SemaphoreType.DMA
    b16, f32 = jnp.bfloat16, jnp.float32
    return pl.pallas_call(
        kernel,
        out_shape=jax.ShapeDtypeStruct((2, TOK, width), b16),
        in_specs=[hbm] * 6,
        out_specs=vmem,
        scratch_shapes=[
            pltpu.VMEM(freq.shape, f32),
            pltpu.VMEM(doc_start.shape, jnp.int32),
            pltpu.VMEM(queries.shape, b16),
            pltpu.VMEM(keys.shape, b16),
            pltpu.VMEM(values.shape, b16),
            pltpu.VMEM((8, 256), jnp.int32),
            pltpu.VMEM((CHUNKS, STRIPES, 2, CT, HD), b16),
            pltpu.VMEM((CHUNKS, 4, 2, CT, HD), b16),
            pltpu.VMEM((4, TOK, WIDE), b16),
            pltpu.VMEM((4, TOK, WIDE), b16),
            pltpu.VMEM((4, 8, 256), jnp.int32),
            pltpu.VMEM((2, TOK, HD), f32),
            pltpu.VMEM((4, TOK, HD), f32),
            pltpu.VMEM((BLOCKS, KEYS, HD), b16),
            pltpu.VMEM((KEYS, HD), b16),
            pltpu.VMEM((BLOCKS + 1, ROWS, 2 * HD), b16),
            pltpu.VMEM((BLOCKS, 2, HD + SUMS, HALF), b16),
            pltpu.VMEM((BUFFERS, HALF, ROWS), f32),
            pltpu.VMEM((BUFFERS, 8, ROWS), f32),
            pltpu.VMEM((BLOCKS + 1, 8, ROWS), f32),
            pltpu.VMEM((BLOCKS, HD + SUMS, ROWS), f32),
            pltpu.VMEM((4, TOK, WIDE), b16),
            pltpu.VMEM((8, TOK, WIDE), b16),
            pltpu.VMEM((2, 2048, width), b16),
            dma((CHUNKS, 7)),
            dma((CHUNKS,)),
            dma((CHUNKS, 3)),
            dma((CHUNKS,)),
            dma((3,)),
            dma((1,)),
            dma((CHUNKS, 2)),
            dma((CHUNKS, 2)),
            dma((CHUNKS, 2)),
            dma((CHUNKS, 2)),
            dma((CHUNKS, 4)),
            dma((CHUNKS, 4)),
            dma((BLOCKS, 7)),
            dma((8, 2)),
            dma((3,)),
            dma((5,)),
        ],
        compiler_params=pltpu.CompilerParams(
            collective_id=0, has_side_effects=True, vmem_limit_bytes=44 * 2**20
        ),
    )(*(pltpu.with_memory_space_constraint(x, pltpu.HBM) for x in (freq, doc_start, queries, keys, values, out_weight)))


def solution(mesh):
    return jax.shard_map(
        local,
        mesh=mesh,
        in_specs=(
            P(None, "ctx", "head"),
            P(None, "ctx", "head"),
            P(None, "ctx", "head"),
            P("ctx"),
            P(None, None, "head"),
        ),
        out_specs=P(None, "ctx", "head"),
        check_vma=False,
    )
```
